32 devices in a mesh: fsdp: 16 (over z, x, core), rep: 2 (over y).
Axes of the slice: x: 2, y: 2, z: 4, core: 2. Of those that a mesh axis runs over, the one named last changes fastest.
Arguments:
- tokens: bfloat16 [32768, 1024], P(('fsdp', 'rep')), may hold values from -6 to 6
- seq_lengths: int32 [64, 4], P(('fsdp', 'rep')), may hold values from 0 to 512, as said below
- out_cotangent: bfloat16 [32768, 1024], P(('fsdp', 'rep')), may hold values from -6 to 6
- project_in: bfloat16 [1024, 3072], P('fsdp'), may hold values from -0.1875 to 0.1875
- project_out: bfloat16 [1024, 1024], P('fsdp'), may hold values from -1.5 to 1.5
- expand: bfloat16 [1024, 4096], P('fsdp'), may hold values from -0.1875 to 0.1875
- contract: bfloat16 [4096, 1024], P('fsdp'), may hold values from -0.09375 to 0.09375
- query_bias: bfloat16 [1024], P('fsdp'), may hold values from -3 to 3
- value_bias: bfloat16 [1024], P('fsdp'), may hold values from -3 to 3
- out_bias: bfloat16 [1024], P('fsdp'), may hold values from -2 to 2
- expand_bias: bfloat16 [4096], P('fsdp'), may hold values from -3 to 3
- contract_bias: bfloat16 [1024], P('fsdp'), may hold values from -2 to 2
- first_gain: bfloat16 [1024], P('fsdp'), may hold values from 0.5 to 1.5
- first_shift: bfloat16 [1024], P('fsdp'), may hold values from -2 to 2
- second_gain: bfloat16 [1024], P('fsdp'), may hold values from 0.5 to 1.5
- second_shift: bfloat16 [1024], P('fsdp'), may hold values from -2 to 2
Outputs:
- layer_output: bfloat16 [32768, 1024], P(('fsdp', 'rep'))
- grad_tokens: bfloat16 [32768, 1024], P(('fsdp', 'rep'))
- grad_project_in: float32 [1024, 3072], P('fsdp')
- grad_project_out: float32 [1024, 1024], P('fsdp')
- grad_expand: float32 [1024, 4096], P('fsdp')
- grad_contract: float32 [4096, 1024], P('fsdp')
- grad_query_bias: float32 [1024], P('fsdp')
- grad_value_bias: float32 [1024], P('fsdp')
- grad_out_bias: float32 [1024], P('fsdp')
- grad_expand_bias: float32 [4096], P('fsdp')
- grad_contract_bias: float32 [1024], P('fsdp')
- grad_first_gain: float32 [1024], P('fsdp')
- grad_first_shift: float32 [1024], P('fsdp')
- grad_second_gain: float32 [1024], P('fsdp')
- grad_second_shift: float32 [1024], P('fsdp')
The draws below stay inside these ranges and needn't reach their ends.
Inputs may be any that keep to these rules, and one draw needn't show every extreme that they name: In each row of seq_lengths the lengths sum to at most 512; rows of a micro-batch past that sum are padding. In every draw one row holds a single sequence of exactly 512 and zeros.
All inputs are finite; a program needn't handle non-finite values.
Results may differ from the reference program's by a relative error of at most 0.015.
Values may be sent and summed in bfloat16 or wider, within the bound.
No kernel may reach another device: no remote copies, remote signals or barrier semaphores. Data moves between devices by JAX's collectives and lax.ppermute only.
A program may use at most 256 MiB of HBM per device.

```python
import jax
import jax.numpy as jnp
from jax import lax

D = 1024
H = 16
HD = 64
FF = 4096
CAP = 512
SLOTS = 4
BUFFERS = 64
ROWS = 32768


def draw_seq_lengths(key, part):
    key = jax.random.fold_in(key, 17)
    fill_key, share_key, pick_key = jax.random.split(key, 3)
    filled = jax.random.randint(fill_key, (BUFFERS, 1), CAP // 4, CAP + 1)
    shares = jax.random.randint(share_key, (BUFFERS, SLOTS), 1, 9)
    lengths = filled * shares // jnp.sum(shares, axis=1, keepdims=True)
    chosen = jax.random.randint(pick_key, (), 0, BUFFERS)
    single = jnp.where(lax.iota(jnp.int32, SLOTS) == 0, CAP, 0)
    picked = lax.iota(jnp.int32, BUFFERS)[:, None] == chosen
    return jnp.where(picked, single[None, :], lengths).astype(jnp.int32)


def level_of(stream_key, extent, cuts, smallest, high):
    level, own = 1.0, jax.random.fold_in(stream_key, 6)
    for dim, parts in cuts:
        steps = jnp.exp(jax.random.uniform(jax.random.fold_in(own, dim), (parts,), jnp.float32, smallest / len(cuts), high / len(cuts)))
        level = level * jnp.repeat(steps, extent[dim] // parts).reshape([-1 if axis == dim else 1 for axis in range(len(extent))])
    return level


def noise(own_key, extent, scale, limit, shards=(), kind=jnp.bfloat16):
    drawn = scale * jax.random.normal(own_key, extent, jnp.float32)
    if shards:
        drawn = drawn * level_of(own_key, extent, shards, -0.22, 0.18)
    return jnp.clip(drawn, -limit, limit).astype(kind)


def setup_inputs(seed: int = 0) -> dict:
    streams_of = jax.random.split(jax.random.key(seed), 17)
    tokens = noise(streams_of[0], (ROWS, D), 1.0, 6.0, ((0, 32),))
    seq_lengths = draw_seq_lengths(jax.random.fold_in(streams_of[16], 71), 0)
    out_cotangent = noise(streams_of[2], (ROWS, D), 1.0, 6.0, ((0, 32),))
    project_in = noise(streams_of[3], (D, 3 * D), D ** -0.5, 0.1875, ((0, 16),))
    project_out = noise(streams_of[4], (D, D), (D // 64) ** -0.5, 1.5, ((0, 16),))
    expand = noise(streams_of[5], (D, FF), D ** -0.5, 0.1875, ((0, 16),))
    contract = noise(streams_of[6], (FF, D), FF ** -0.5, 0.09375, ((0, 16),))
    query_bias = noise(streams_of[7], (D,), 0.5, 3.0, ((0, 16),))
    value_bias = noise(streams_of[8], (D,), 0.5, 3.0, ((0, 16),))
    out_bias = noise(streams_of[9], (D,), 0.3, 2.0, ((0, 16),))
    expand_bias = noise(streams_of[10], (FF,), 0.5, 3.0, ((0, 16),))
    contract_bias = noise(streams_of[11], (D,), 0.3, 2.0, ((0, 16),))
    first_gain = jnp.clip(1.0 + 0.1 * jax.random.normal(streams_of[12], (D,), jnp.float32), 0.5, 1.5).astype(jnp.bfloat16)
    first_shift = noise(streams_of[13], (D,), 0.3, 2.0, ((0, 16),))
    second_gain = jnp.clip(1.0 + 0.1 * jax.random.normal(streams_of[14], (D,), jnp.float32), 0.5, 1.5).astype(jnp.bfloat16)
    second_shift = noise(streams_of[15], (D,), 0.3, 2.0, ((0, 16),))
    return {"tokens": tokens, "seq_lengths": seq_lengths, "out_cotangent": out_cotangent, "project_in": project_in, "project_out": project_out, "expand": expand, "contract": contract, "query_bias": query_bias, "value_bias": value_bias, "out_bias": out_bias, "expand_bias": expand_bias, "contract_bias": contract_bias, "first_gain": first_gain, "first_shift": first_shift, "second_gain": second_gain, "second_shift": second_shift}


EPSILON = 1e-12
SCALE = 0.125
PRECISE = lax.Precision.HIGHEST

@jax.custom_vjp
def low(v):
    return lax.optimization_barrier(v.astype(jnp.bfloat16)).astype(jnp.float32)

@jax.custom_vjp
def low_back(v):
    return v

def low_keep(v):
    return (low(v), None)

def low_pass(kept, grad):
    return (grad,)

def back_keep(v):
    return (v, None)

def back_low(kept, grad):
    return (low(grad),)
low.defvjp(low_keep, low_pass)
low_back.defvjp(back_keep, back_low)

def segment_mask(row_lengths, row_count):
    boundary = jnp.cumsum(row_lengths.astype(jnp.int32), dtype=jnp.int32)
    position = lax.iota(jnp.int32, row_count)
    slot_index = lax.optimization_barrier(jnp.sum((position[:, None] >= boundary[None, :]).astype(jnp.int32), axis=1))
    inside = slot_index < row_lengths.shape[0]
    together = (slot_index[:, None] == slot_index[None, :]) & inside[None, :]
    return together | (position[:, None] == position[None, :])

def normalize(summed, gain, shift):
    centre = lax.optimization_barrier(jnp.mean(summed, axis=-1, keepdims=True))
    centred = summed - centre
    spread = lax.optimization_barrier(jnp.mean(centred * centred, axis=-1, keepdims=True))
    return centred * lax.rsqrt(spread + EPSILON) * gain + shift

def forward(block_rows, allowed, parameters):
    project_in, project_out, expand, contract, query_bias, value_bias, out_bias, expand_bias, contract_bias, first_gain, first_shift, second_gain, second_shift = parameters
    row_count = block_rows.shape[0]
    offsets = jnp.concatenate([query_bias, jnp.zeros_like(query_bias), value_bias])
    projected = low(low_back(jnp.dot(block_rows, project_in, precision=PRECISE) + offsets))
    queries = projected[:, :D].reshape(row_count, H, HD)
    keyed = projected[:, D:2 * D].reshape(row_count, H, HD)
    valued = projected[:, 2 * D:].reshape(row_count, H, HD)
    scores = low_back(jnp.einsum('qhd,khd->hqk', queries, keyed, precision=PRECISE) * SCALE)
    scores = jnp.where(allowed[None], scores, -1e+30)
    highest = lax.optimization_barrier(jnp.max(scores, axis=-1, keepdims=True))
    weights = jnp.exp(scores - highest)
    attention = weights / lax.optimization_barrier(jnp.sum(weights, axis=-1, keepdims=True))
    attended = jnp.einsum('hqk,khd->qhd', low(attention), valued, precision=PRECISE).reshape(row_count, D)
    attended = low(low_back(attended))
    branch = low_back(jnp.dot(attended, project_out, precision=PRECISE) + out_bias)
    first_norm = normalize(block_rows + branch, first_gain, first_shift)
    expanded = low_back(jnp.dot(low(first_norm), expand, precision=PRECISE) + expand_bias)
    active = low(jax.nn.gelu(expanded, approximate=False))
    contracted = low_back(jnp.dot(active, contract, precision=PRECISE) + contract_bias)
    return normalize(first_norm + contracted, second_gain, second_shift)

def reference(tokens, seq_lengths, out_cotangent, project_in, project_out, expand, contract, query_bias, value_bias, out_bias, expand_bias, contract_bias, first_gain, first_shift, second_gain, second_shift):
    parameters = tuple((item.astype(jnp.float32) for item in (project_in, project_out, expand, contract, query_bias, value_bias, out_bias, expand_bias, contract_bias, first_gain, first_shift, second_gain, second_shift)))
    blocks = tokens.reshape(BUFFERS, CAP, D)
    cotangents = out_cotangent.reshape(BUFFERS, CAP, D)

    def one_block(totals, carried):
        block_rows, block_cot, block_lengths = carried
        allowed = segment_mask(block_lengths, CAP)
        result, pull = jax.vjp(lambda rows_in, weights_in: forward(rows_in, allowed, weights_in), block_rows.astype(jnp.float32), parameters)
        grad_rows, grad_weights = pull(block_cot.astype(jnp.float32))
        totals = jax.tree.map(lambda left, right: left + right, totals, grad_weights)
        return (totals, (result.astype(jnp.bfloat16), grad_rows.astype(jnp.bfloat16)))
    start = jax.tree.map(jnp.zeros_like, parameters)
    totals, (outputs, grad_rows) = lax.scan(one_block, start, (blocks, cotangents, seq_lengths))
    return (outputs.reshape(BUFFERS * CAP, D), grad_rows.reshape(BUFFERS * CAP, D), totals[0], totals[1], totals[2], totals[3], totals[4], totals[5], totals[6], totals[7], totals[8], totals[9], totals[10], totals[11], totals[12])
```

```python
import functools

import jax
import jax.numpy as jnp
from jax import lax
from jax.experimental import pallas as pl
from jax.experimental.pallas import tpu as pltpu
from jax.sharding import PartitionSpec as P

H = 16
HD = 64
SLOTS = 4
CAP = 512
EPSILON = 1e-12
SCALE = 0.125
BIG = 1e30
LOW = jnp.bfloat16
F32 = jnp.float32
VMEM_LIMIT = 60 * 1024 * 1024
ANY = pl.BlockSpec(memory_space=pl.ANY)
OWN, ACROSS, OTHER, CORNER = (0, 0), (1, 0), (0, 1), (1, 1)
GROUPS = (OWN, ACROSS, OTHER, CORNER)


def params(limit=VMEM_LIMIT):
    return pltpu.CompilerParams(vmem_limit_bytes=limit, dimension_semantics=("arbitrary",))


def dot(left, right, over):
    return lax.dot_general(left, right, ((over[:1], over[1:]), ((), ())), preferred_element_type=F32)


def nn(left, right):
    return dot(left, right, (1, 0))


def nt(left, right):
    return dot(left, right, (1, 1))


def tn(left, right):
    return dot(left, right, (0, 0))


class Plan:
    def __init__(self, shards, copies):
        self.shards, self.copies = shards, copies
        self.split = shards == 16 and copies == 2

    def flip(self, value, bits):
        return lax.ppermute(value, "fsdp", [(i, i ^ bits) for i in range(self.shards)])

    def other_copy(self, value):
        return lax.ppermute(value, "rep", [(0, 1), (1, 0)])

    def gather(self, shard):
        if not self.split:
            return [lax.all_gather(shard, "fsdp", axis=0, tiled=True)]
        half = shard.shape[0] // 2
        rep = lax.axis_index("rep")
        own = lax.dynamic_slice_in_dim(shard, rep * half, half, 0)
        own = jnp.concatenate([own] + [self.flip(own, 4 * k) for k in (1, 2, 3)], axis=0)
        across = self.flip(own, 2)
        other = self.other_copy(own)
        corner_a = self.flip(other[: 2 * half], 2)
        corner_b = self.other_copy(across[2 * half :])
        pieces = [own, across, other, corner_a, corner_b]
        return pieces + [self.flip(piece, 1) for piece in pieces]

    def piece_list(self):
        out = []
        for core in (0, 1):
            for piece, (group, first, count) in enumerate(
                ((OWN, 0, 4), (ACROSS, 0, 4), (OTHER, 0, 4), (CORNER, 0, 2), (CORNER, 2, 2))
            ):
                for k in range(count):
                    out.append((piece + 5 * core, k, first + k, group[0], core, group[1]))
        return out

    def scatter(self, mine, theirs):
        half = mine.shape[0] // 16
        rep = lax.axis_index("rep")
        got = self.flip(theirs, 1)

        def part(group, first=0, count=4):
            start = (GROUPS.index(group) * 4 + first) * half
            stop = start + count * half
            return mine[start:stop].astype(F32) + got[start:stop].astype(F32)

        corner_a = self.flip(part(CORNER, 0, 2).astype(LOW), 2)
        corner_b = self.other_copy(part(CORNER, 2, 2).astype(LOW))
        other = jnp.concatenate(
            [part(OTHER, 0, 2) + corner_a.astype(F32), part(OTHER, 2, 2)], axis=0
        ).astype(LOW)
        across = jnp.concatenate(
            [part(ACROSS, 0, 2), part(ACROSS, 2, 2) + corner_b.astype(F32)], axis=0
        ).astype(LOW)
        own = part(OWN) + self.flip(across, 2).astype(F32) + self.other_copy(other).astype(F32)
        total = own[:half]
        low = own.astype(LOW)
        for k in (1, 2, 3):
            total = total + self.flip(low[k * half : (k + 1) * half], 4 * k).astype(F32)
        total = total.astype(LOW)
        away = self.other_copy(total)
        first = jnp.where(rep == 0, total, away)
        second = jnp.where(rep == 0, away, total)
        return jnp.concatenate([first, second], axis=0).astype(F32)


def place():
    shard = lax.axis_index("fsdp")
    return jnp.stack([shard // 4, (shard // 2) % 2, shard % 2, lax.axis_index("rep")]).astype(jnp.int32)


def load_copies(plan, at, pieces, target, sems, rows):
    if not plan.split:
        return [pltpu.make_async_copy(pieces[0], target, sems)]
    half = rows // plan.shards // 2
    copies = []
    for piece, k, dz, dx, dc, dy in plan.piece_list():
        shard = (at[0] ^ dz) * 4 + (at[1] ^ dx) * 2 + (at[2] ^ dc)
        row = pl.multiple_of(shard * 2 * half + (at[3] ^ dy) * half, half)
        copies.append(
            pltpu.make_async_copy(
                pieces[piece].at[pl.ds(k * half, half)], target.at[pl.ds(row, half)], sems
            )
        )
    return copies


def fetch(plan, at, groups, sems):
    started = []
    for index, (pieces, target, rows) in enumerate(groups):
        for copy in load_copies(plan, at, pieces, target, sems.at[index], rows):
            copy.start()
            started.append(copy)
    for copy in started:
        copy.wait()


def project_kernel(plan, count, at, rows_ref, bias_ref, *refs):
    pieces, (out_ref, weight, sems) = refs[:count], refs[count:]

    @pl.when(pl.program_id(0) == 0)
    def _():
        fetch(plan, at, [(pieces, weight, weight.shape[0])], sems)

    out_ref[...] = (nn(rows_ref[...], weight[...]) + bias_ref[0:1].astype(F32)).astype(LOW)


def project(plan, at, rows, bias, pieces, depth, width, tile=256):
    count = len(pieces)
    return pl.pallas_call(
        functools.partial(project_kernel, plan, count),
        out_shape=jax.ShapeDtypeStruct((rows.shape[0], width), LOW),
        grid_spec=pltpu.PrefetchScalarGridSpec(
            num_scalar_prefetch=1,
            grid=(rows.shape[0] // tile,),
            in_specs=[
                pl.BlockSpec((tile, depth), lambda i, at: (i, 0)),
                pl.BlockSpec((1, width), lambda i, at: (0, 0)),
            ]
            + [ANY] * count,
            out_specs=pl.BlockSpec((tile, width), lambda i, at: (i, 0)),
            scratch_shapes=[pltpu.VMEM((depth, width), LOW), pltpu.SemaphoreType.DMA((1,))],
        ),
        compiler_params=params(),
        cost_estimate=pl.CostEstimate(
            flops=2 * rows.shape[0] * depth * width, bytes_accessed=2 * depth * width, transcendentals=0
        ),
    )(at, rows, bias, *pieces)


def slot_rows(lengths_ref, block, row_count):
    along = lax.broadcasted_iota(jnp.int32, (1, row_count), 1)
    down = lax.broadcasted_iota(jnp.int32, (row_count, 1), 0)
    bound, lane_slot, row_slot = 0, jnp.zeros_like(along), jnp.zeros_like(down)
    for slot in range(SLOTS):
        bound = bound + lengths_ref[block, slot]
        lane_slot = lane_slot + (along >= bound).astype(jnp.int32)
        row_slot = row_slot + (down >= bound).astype(jnp.int32)
    return lane_slot, row_slot


def query_rows(lane_slot):
    line = lax.broadcasted_iota(jnp.int32, (8, lane_slot.shape[1]), 0)
    return jnp.where(line == lane_slot, -BIG, 0.0)


def key_columns(row_slot, offset):
    column = lax.broadcasted_iota(jnp.int32, (row_slot.shape[0], 128), 1) - offset
    barred = (column >= 0) & (column <= SLOTS) & ((column != row_slot) | (row_slot == SLOTS))
    return jnp.where(barred, 1.0, 0.0).astype(LOW)


def attend_kernel(lengths_ref, q_ref, k_ref, v_ref, out_ref, log_ref):
    block = pl.program_id(0) // (H // 2)
    row_count = q_ref.shape[0]
    lane_slot, row_slot = slot_rows(lengths_ref, block, row_count)
    inside = lane_slot < SLOTS
    lane = lax.broadcasted_iota(jnp.int32, (row_count, 128), 1)
    barred = query_rows(lane_slot).astype(LOW)
    padded = jnp.concatenate([barred, jnp.zeros((HD - 8, row_count), LOW)], axis=0)
    q_turned = (q_ref[...].astype(F32) * SCALE).T.astype(LOW)
    v_turned = v_ref[...].astype(F32).T
    v_low = v_turned.astype(LOW)
    ones = jnp.ones((16, row_count), LOW)
    results = []
    for head in range(2):
        own = (lane < HD) if head == 0 else (lane >= HD)
        keyed = jnp.where(own, k_ref[...], key_columns(row_slot, HD * (1 - head)))
        half = q_turned[head * HD : (head + 1) * HD]
        query = jnp.concatenate([half, padded] if head == 0 else [padded, half], axis=0)
        scores = nn(keyed, query)
        highest = jnp.max(scores, axis=0, keepdims=True)
        weights = jnp.exp(scores - highest)
        low = weights.astype(LOW)
        values = jnp.concatenate([v_low[head * HD : (head + 1) * HD], ones], axis=0)
        mixed = nn(values, low)
        total = mixed[HD : HD + 1]
        result = mixed[:HD] / total
        results.append(jnp.where(inside, result, v_turned[head * HD : (head + 1) * HD]))
        log_ref[0, head : head + 1] = jnp.where(inside, highest + jnp.log(total), BIG)
    out_ref[...] = jnp.concatenate(results, axis=0).T.astype(LOW)


def attend(lengths, projected):
    rows = projected.shape[0]
    blocks, pairs = rows // CAP, H // 2
    width = H * HD

    def column(part):
        return pl.BlockSpec((CAP, 128), lambda i, n: (i // pairs, part * pairs + i % pairs))

    return pl.pallas_call(
        attend_kernel,
        out_shape=(
            jax.ShapeDtypeStruct((rows, width), LOW),
            jax.ShapeDtypeStruct((blocks * pairs, 8, CAP), F32),
        ),
        grid_spec=pltpu.PrefetchScalarGridSpec(
            num_scalar_prefetch=1,
            grid=(blocks * pairs,),
            in_specs=[column(0), column(1), column(2)],
            out_specs=(column(0), pl.BlockSpec((1, 8, CAP), lambda i, n: (i, 0, 0))),
        ),
        compiler_params=params(),
        cost_estimate=pl.CostEstimate(
            flops=4 * 4 * rows * CAP * width, bytes_accessed=8 * rows * width, transcendentals=rows * CAP * H
        ),
    )(lengths, projected, projected, projected)


def three(value):
    first = value.astype(LOW).astype(F32)
    rest = value - first
    second = rest.astype(LOW).astype(F32)
    return first, second, rest - second


def attend_back_kernel(lengths_ref, q_ref, k_ref, v_ref, att_ref, grad_ref, log_ref, dq_ref, dk_ref, dv_ref):
    block = pl.program_id(0) // (H // 2)
    row_count = q_ref.shape[0]
    lane_slot, row_slot = slot_rows(lengths_ref, block, row_count)
    outside = row_slot >= SLOTS
    lane = lax.broadcasted_iota(jnp.int32, (row_count, 128), 1)
    barred = query_rows(lane_slot)
    q_scaled = (q_ref[...].astype(F32) * SCALE)
    q_turned = q_scaled.T.astype(LOW)
    k_scaled = k_ref[...].astype(F32) * SCALE
    k_turned = k_scaled.T.astype(LOW)
    grads = grad_ref[...]
    grad_wide = grads.astype(F32)
    grad_turned = grad_wide.T
    mixed = grad_turned * att_ref[...].astype(F32).T
    grad_turned = grad_turned.astype(LOW)
    q_low = q_scaled.astype(LOW)
    line = lax.broadcasted_iota(jnp.int32, (8, row_count), 0)
    none = jnp.zeros((HD - 16, row_count), F32)

    def lines(value):
        first, second, third = three(value)
        return jnp.where(
            line == 0, -first, jnp.where(line == 1, -second, jnp.where(line == 2, -third, 0.0))
        )

    dqs, dks, dvs = [], [], []
    for head in range(2):
        own = (lane < HD) if head == 0 else (lane >= HD)
        start = HD * (1 - head)
        unit = (lane >= start + 8) & (lane < start + 11)
        keyed = jnp.where(own, k_ref[...], jnp.where(unit, jnp.ones((), LOW), key_columns(row_slot, start)))
        valued = jnp.where(own, v_ref[...], jnp.where(unit, jnp.ones((), LOW), jnp.zeros((), LOW)))
        extra = jnp.concatenate([barred, lines(log_ref[0, head : head + 1]), none], axis=0).astype(LOW)
        half = slice(head * HD, (head + 1) * HD)
        query = jnp.concatenate([q_turned[half], extra] if head == 0 else [extra, q_turned[half]], axis=0)
        weights = jnp.exp(nn(keyed, query))
        inner = jnp.sum(mixed[half], axis=0, keepdims=True)
        extra = jnp.concatenate([jnp.zeros_like(barred), lines(inner), none], axis=0).astype(LOW)
        grad = jnp.concatenate([grad_turned[half], extra] if head == 0 else [extra, grad_turned[half]], axis=0)
        moved = (weights * nn(valued, grad)).astype(LOW)
        dvs.append(nn(weights.astype(LOW), grads))
        dks.append(nn(moved, q_low))
        dqs.append(nn(k_turned[half], moved))
    dq_ref[...] = jnp.concatenate(dqs, axis=0).T.astype(LOW)
    dk_ref[...] = jnp.where(lane < HD, dks[0], dks[1]).astype(LOW)
    dv = jnp.where(lane < HD, dvs[0], dvs[1])
    dv_ref[...] = jnp.where(outside, dv + grad_wide, dv).astype(LOW)


def attend_back(lengths, projected, attended, grad_attended, logs):
    rows = projected.shape[0]
    blocks, pairs = rows // CAP, H // 2
    width = H * HD

    def column(part):
        return pl.BlockSpec((CAP, 128), lambda i, n: (i // pairs, part * pairs + i % pairs))

    return pl.pallas_call(
        attend_back_kernel,
        out_shape=(jax.ShapeDtypeStruct((rows, width), LOW),) * 3,
        grid_spec=pltpu.PrefetchScalarGridSpec(
            num_scalar_prefetch=1,
            grid=(blocks * pairs,),
            in_specs=[column(0), column(1), column(2), column(0), column(0)]
            + [pl.BlockSpec((1, 8, CAP), lambda i, n: (i, 0, 0))],
            out_specs=(column(0),) * 3,
        ),
        compiler_params=params(),
        cost_estimate=pl.CostEstimate(
            flops=10 * 4 * rows * CAP * width, bytes_accessed=16 * rows * width, transcendentals=rows * CAP * H
        ),
    )(lengths, projected, projected, projected, attended, grad_attended, logs)


def norm(values):
    centre = jnp.mean(values, axis=-1, keepdims=True)
    centred = values - centre
    scale = lax.rsqrt(jnp.mean(centred * centred, axis=-1, keepdims=True) + EPSILON)
    return centred * scale, scale


def norm_back(grad, normal, scale):
    return scale * (
        grad
        - jnp.mean(grad, axis=-1, keepdims=True)
        - normal * jnp.mean(grad * normal, axis=-1, keepdims=True)
    )


ROOT_HALF = 0.7071067811865476
ROOT_TAU = 0.3989422804014327


def middle_kernel(plan, count, chunk, at, rows_ref, att_ref, cot_ref, small_ref, wide_ref, *refs):
    out_pieces, expand_pieces, contract_pieces = (refs[i * count : (i + 1) * count] for i in range(3))
    (
        result_ref, active_ref, first_ref, second_ref, expanded_ref, branch_ref, grad_att_ref,
        sums_ref, wide_sums_ref, w_out, w_expand, w_contract, slope, sems,
    ) = refs[3 * count :]
    depth, hidden = w_expand.shape

    @pl.when(pl.program_id(0) == 0)
    def _():
        fetch(
            plan,
            at,
            [(out_pieces, w_out, depth), (expand_pieces, w_expand, depth), (contract_pieces, w_contract, hidden)],
            sems,
        )
        sums_ref[...] = jnp.zeros_like(sums_ref)
        wide_sums_ref[...] = jnp.zeros_like(wide_sums_ref)

    def small(index):
        return small_ref[index : index + 1].astype(F32)

    def add(index, value):
        sums_ref[index : index + 1] += jnp.sum(value, axis=0, keepdims=True)

    out_bias, contract_bias, gain_one, shift_one, gain_two, shift_two = (small(i) for i in range(6))
    residual = rows_ref[...].astype(F32) + nn(att_ref[...], w_out[...]) + out_bias
    normal_one, scale_one = norm(residual)
    first = normal_one * gain_one + shift_one
    low = first.astype(LOW)
    first_ref[...] = low
    total = first + contract_bias
    for start in range(0, hidden, chunk):
        span = slice(start, start + chunk)
        wide = nn(low, w_expand[:, span]) + wide_ref[0:1, span].astype(F32)
        cumulative = 0.5 * (1.0 + lax.erf(wide * ROOT_HALF))
        active = (wide * cumulative).astype(LOW)
        slope[:, span] = cumulative + wide * (ROOT_TAU * jnp.exp(-0.5 * wide * wide))
        active_ref[:, span] = active
        total = total + nn(active, w_contract[span])
    normal_two, scale_two = norm(total)
    result_ref[...] = (normal_two * gain_two + shift_two).astype(LOW)
    cot = cot_ref[...].astype(F32)
    add(4, cot * normal_two)
    add(5, cot)
    second = norm_back(cot * gain_two, normal_two, scale_two)
    second_low = second.astype(LOW)
    second_ref[...] = second_low
    add(1, second_low.astype(F32))
    total = second
    for start in range(0, hidden, chunk):
        span = slice(start, start + chunk)
        grad = (nt(second_low, w_contract[span]) * slope[:, span]).astype(LOW)
        expanded_ref[:, span] = grad
        wide_sums_ref[0:1, span] += jnp.sum(grad.astype(F32), axis=0, keepdims=True)
        total = total + nt(grad, w_expand[:, span])
    add(2, total * normal_one)
    add(3, total)
    branch = norm_back(total * gain_one, normal_one, scale_one)
    branch_low = branch.astype(LOW)
    branch_ref[...] = branch_low
    add(0, branch_low.astype(F32))
    grad_att_ref[...] = nt(branch_low, w_out[...]).astype(LOW)


def middle(plan, at, rows, attended, cot, small, wide, out_pieces, expand_pieces, contract_pieces, tile=256, chunk=1024):
    count = len(out_pieces)
    height, depth = rows.shape
    hidden = wide.shape[1]

    def tiled(width):
        return pl.BlockSpec((tile, width), lambda i, at: (i, 0))

    def whole(height, width):
        return pl.BlockSpec((height, width), lambda i, at: (0, 0))

    return pl.pallas_call(
        functools.partial(middle_kernel, plan, count, chunk),
        out_shape=(
            jax.ShapeDtypeStruct((height, depth), LOW),
            jax.ShapeDtypeStruct((height, hidden), LOW),
            jax.ShapeDtypeStruct((height, depth), LOW),
            jax.ShapeDtypeStruct((height, depth), LOW),
            jax.ShapeDtypeStruct((height, hidden), LOW),
            jax.ShapeDtypeStruct((height, depth), LOW),
            jax.ShapeDtypeStruct((height, depth), LOW),
            jax.ShapeDtypeStruct((8, depth), F32),
            jax.ShapeDtypeStruct((8, hidden), F32),
        ),
        grid_spec=pltpu.PrefetchScalarGridSpec(
            num_scalar_prefetch=1,
            grid=(height // tile,),
            in_specs=[tiled(depth), tiled(depth), tiled(depth), whole(8, depth), whole(1, hidden)]
            + [ANY] * (3 * count),
            out_specs=(
                tiled(depth), tiled(hidden), tiled(depth), tiled(depth), tiled(hidden), tiled(depth),
                tiled(depth), whole(8, depth), whole(8, hidden),
            ),
            scratch_shapes=[
                pltpu.VMEM((depth, depth), LOW),
                pltpu.VMEM((depth, hidden), LOW),
                pltpu.VMEM((hidden, depth), LOW),
                pltpu.VMEM((tile, hidden), F32),
                pltpu.SemaphoreType.DMA((3,)),
            ],
        ),
        compiler_params=params(),
        cost_estimate=pl.CostEstimate(
            flops=4 * height * depth * (depth + 2 * hidden),
            bytes_accessed=2 * depth * (depth + 2 * hidden) + 4 * height * (depth * 4 + hidden),
            transcendentals=2 * height * hidden,
        ),
    )(at, rows, attended, cot, small, wide, *out_pieces, *expand_pieces, *contract_pieces)


def outer_kernel(plan, rows, count, at, left_ref, *refs):
    rights, outs = refs[:count], refs[count:]
    tile = left_ref.shape[1]
    step = pl.program_id(0)
    turned = left_ref[...].T
    start = 0
    for right in rights:
        span = slice(start, start + right.shape[1])
        start += right.shape[1]
        result = nn(turned, right[...])
        if not plan.split:
            outs[0][:, span] = result.astype(LOW)
            continue
        half = rows // plan.shards // 2
        result = result.astype(LOW)
        for j in range(tile // half):
            shard = step * (tile // half // 2) + j // 2
            group = ((shard // 2) % 2 ^ at[1]) + 2 * (j % 2 ^ at[3])
            row = pl.multiple_of((group * 4 + ((shard // 4) ^ at[0])) * half, half)
            same = at[2] == (j // 2) % 2

            @pl.when(same)
            def _(j=j, row=row, result=result, span=span):
                outs[0][pl.ds(row, half), span] = result[j * half : (j + 1) * half]

            @pl.when(jnp.logical_not(same))
            def _(j=j, row=row, result=result, span=span):
                outs[1][pl.ds(row, half), span] = result[j * half : (j + 1) * half]


def outer(plan, at, left, rights, tile):
    height, rows = left.shape
    width = sum(right.shape[1] for right in rights)
    if plan.split:
        out_shape = (jax.ShapeDtypeStruct((rows // 2, width), LOW),) * 2
        out_specs = (pl.BlockSpec((rows // 2, width), lambda i, at: (0, 0)),) * 2
    else:
        out_shape = (jax.ShapeDtypeStruct((rows, width), LOW),)
        out_specs = (pl.BlockSpec((tile, width), lambda i, at: (i, 0)),)
    return pl.pallas_call(
        functools.partial(outer_kernel, plan, rows, len(rights)),
        out_shape=out_shape,
        grid_spec=pltpu.PrefetchScalarGridSpec(
            num_scalar_prefetch=1,
            grid=(rows // tile,),
            in_specs=[pl.BlockSpec((height, tile), lambda i, at: (0, i))]
            + [pl.BlockSpec(right.shape, lambda i, at: (0, 0)) for right in rights],
            out_specs=out_specs,
        ),
        compiler_params=params(),
        cost_estimate=pl.CostEstimate(
            flops=2 * height * rows * width, bytes_accessed=2 * (rows * width + height * (rows + width)), transcendentals=0
        ),
    )(at, left, *rights)


def reduce_outer(plan, parts):
    if plan.split:
        return plan.scatter(*parts)
    owned = lax.psum_scatter(parts[0], "fsdp", scatter_dimension=0, tiled=True)
    return lax.psum(owned.astype(LOW), "rep").astype(F32)


def back_kernel(plan, count, at, branch_ref, dq_ref, dk_ref, dv_ref, *refs):
    pieces, (out_ref, sums_ref, weight, sems) = refs[:count], refs[count:]
    width = dq_ref.shape[1]

    @pl.when(pl.program_id(0) == 0)
    def _():
        fetch(plan, at, [(pieces, weight, weight.shape[0])], sems)
        sums_ref[...] = jnp.zeros_like(sums_ref)

    total = branch_ref[...].astype(F32)
    for index, ref in enumerate((dq_ref, dk_ref, dv_ref)):
        total = total + nt(ref[...], weight[:, index * width : (index + 1) * width])
    out_ref[...] = total.astype(LOW)
    sums_ref[0:1] += jnp.sum(dq_ref[...].astype(F32), axis=0, keepdims=True)
    sums_ref[1:2] += jnp.sum(dv_ref[...].astype(F32), axis=0, keepdims=True)


def back(plan, at, branch, dq, dk, dv, pieces, tile=256):
    count = len(pieces)
    height, depth = branch.shape
    width = dq.shape[1]
    tiled = pl.BlockSpec((tile, depth), lambda i, at: (i, 0))
    return pl.pallas_call(
        functools.partial(back_kernel, plan, count),
        out_shape=(jax.ShapeDtypeStruct((height, depth), LOW), jax.ShapeDtypeStruct((8, width), F32)),
        grid_spec=pltpu.PrefetchScalarGridSpec(
            num_scalar_prefetch=1,
            grid=(height // tile,),
            in_specs=[tiled] * 4 + [ANY] * count,
            out_specs=(tiled, pl.BlockSpec((8, width), lambda i, at: (0, 0))),
            scratch_shapes=[pltpu.VMEM((depth, 3 * width), LOW), pltpu.SemaphoreType.DMA((1,))],
        ),
        compiler_params=params(),
        cost_estimate=pl.CostEstimate(
            flops=6 * height * depth * width, bytes_accessed=6 * depth * width + 10 * height * depth, transcendentals=0
        ),
    )(at, branch, dq, dk, dv, *pieces)


def body(
    tokens, seq_lengths, out_cotangent, project_in, project_out, expand, contract,
    query_bias, value_bias, out_bias, expand_bias, contract_bias,
    first_gain, first_shift, second_gain, second_shift,
    *, shards, copies,
):
    plan = Plan(shards, copies)
    at = place()
    depth = tokens.shape[1]
    hidden = expand.shape[1]
    part, wide_part = query_bias.shape[0], expand_bias.shape[0]
    vectors = (query_bias, value_bias, out_bias, contract_bias, first_gain, first_shift, second_gain, second_shift)
    packed = jnp.concatenate(vectors + (expand_bias,))[None]
    packed = lax.all_gather(packed, "fsdp", axis=0, tiled=True)
    small = [packed[:, i * part : (i + 1) * part].reshape(-1) for i in range(8)]
    wide = packed[:, 8 * part :].reshape(1, -1)
    bias = jnp.concatenate([small[0], jnp.zeros_like(small[0]), small[1]])[None]
    table = jnp.stack(small[2:] + [jnp.zeros_like(small[0])] * 2)

    in_pieces = plan.gather(project_in)
    out_pieces = plan.gather(project_out)
    expand_pieces = plan.gather(expand)
    contract_pieces = plan.gather(contract)

    projected = project(plan, at, tokens, bias, in_pieces, depth, project_in.shape[1])
    attended, logs = attend(seq_lengths, projected)
    result, active, first, second, grad_expanded, branch, grad_attended, sums, wide_sums = middle(
        plan, at, tokens, attended, out_cotangent, table, wide, out_pieces, expand_pieces, contract_pieces
    )
    grad_contract = reduce_outer(plan, outer(plan, at, active, [second], 512))
    grad_expand = reduce_outer(plan, outer(plan, at, first, [grad_expanded], 256))
    grad_project_out = reduce_outer(plan, outer(plan, at, attended, [branch], 256))
    dq, dk, dv = attend_back(seq_lengths, projected, attended, grad_attended, logs)
    grad_project_in = reduce_outer(plan, outer(plan, at, tokens, [dq, dk, dv], 256))
    grad_tokens, back_sums = back(plan, at, branch, dq, dk, dv, in_pieces)

    vector_sums = jnp.concatenate([back_sums[:2], sums[:6]], axis=0)
    by_owner = jnp.concatenate(
        [
            vector_sums.reshape(8, shards, part).transpose(1, 0, 2).reshape(shards, 8 * part),
            wide_sums[0].reshape(shards, wide_part),
        ],
        axis=1,
    )
    owned = lax.psum_scatter(by_owner, "fsdp", scatter_dimension=0, tiled=True)
    owned = lax.psum(owned, "rep")[0]
    vector = [owned[i * part : (i + 1) * part] for i in range(8)]
    grad_query, grad_value, grad_out, grad_down, gain_one, shift_one, gain_two, shift_two = vector
    return (
        result, grad_tokens, grad_project_in, grad_project_out, grad_expand, grad_contract,
        grad_query, grad_value, grad_out, owned[8 * part :], grad_down,
        gain_one, shift_one, gain_two, shift_two,
    )


def solution(mesh):
    split, row, vector = P(("fsdp", "rep"), None), P("fsdp", None), P("fsdp")
    return jax.shard_map(
        functools.partial(body, shards=mesh.shape["fsdp"], copies=mesh.shape["rep"]),
        mesh=mesh,
        in_specs=(split,) * 3 + (row,) * 4 + (vector,) * 9,
        out_specs=(split,) * 2 + (row,) * 4 + (vector,) * 9,
        check_vma=False,
    )
```

```python
import functools

import jax
import jax.numpy as jnp
from jax import lax
from jax.experimental import pallas as pl
from jax.experimental.pallas import tpu as pltpu
from jax.sharding import PartitionSpec as P

H = 16
HD = 64
SLOTS = 4
CAP = 512
EPSILON = 1e-12
SCALE = 0.125
BIG = 1e30
EXTRA = 128
HASTE = 1
LOW = jnp.bfloat16
F32 = jnp.float32
VMEM_LIMIT = 60 * 1024 * 1024
ANY = pl.BlockSpec(memory_space=pl.ANY)
OWN, ACROSS, OTHER, CORNER = (0, 0), (1, 0), (0, 1), (1, 1)
GROUPS = (OWN, ACROSS, OTHER, CORNER)


def params(limit=VMEM_LIMIT):
    return pltpu.CompilerParams(vmem_limit_bytes=limit, dimension_semantics=("arbitrary",))


def cost(flops, slow=2):
    return pl.CostEstimate(flops=slow * flops // HASTE, bytes_accessed=slow * flops // HASTE // 320, transcendentals=0)


def later(kernel, prefetch, after):
    def run(*refs):
        kernel(*refs[:prefetch], *refs[prefetch + len(after) :])

    return run


def dot(left, right, over):
    return lax.dot_general(left, right, ((over[:1], over[1:]), ((), ())), preferred_element_type=F32)


def nn(left, right):
    return dot(left, right, (1, 0))


def nt(left, right):
    return dot(left, right, (1, 1))


def tn(left, right):
    return dot(left, right, (0, 0))


def pinned(at, *values):
    for value in values:
        sample = jnp.clip(value[(0,) * value.ndim].astype(F32), -1.0, 1.0).astype(jnp.int32)
        at = at + jnp.minimum(jnp.abs(sample), 0)
    return at


class Plan:
    def __init__(self, shards, copies):
        self.shards, self.copies = shards, copies
        self.split = shards == 16 and copies == 2

    def flip(self, value, bits):
        return lax.ppermute(value, "fsdp", [(i, i ^ bits) for i in range(self.shards)])

    def other_copy(self, value):
        return lax.ppermute(value, "rep", [(0, 1), (1, 0)])


    def gather_z(self, at, shard, early=False):
        half = shard.shape[0] // 2
        own = lax.dynamic_slice_in_dim(shard, at[3] * half, half, 0)
        beside = self.flip(shard, 2) if early else None
        return beside, [self.flip(own, 4 * k) for k in (1, 2, 3)]

    def gather_xy(self, at, shard, far, early=False):
        half = shard.shape[0] // 2
        far = jnp.concatenate([part + at[4].astype(LOW) for part in far], axis=0)
        own = lax.dynamic_slice_in_dim(shard, at[3] * half, half, 0)
        across = far if early else jnp.concatenate([own, far], axis=0)
        return far, self.flip(across, 2), self.other_copy(far)

    def gather_corner(self, at, shard, across, other, early=False):
        half = shard.shape[0] // 2
        left = lax.dynamic_slice_in_dim(other, at[4], half, 0)
        if not early:
            left = jnp.concatenate([lax.dynamic_slice_in_dim(shard, (1 - at[3]) * half, half, 0), left], axis=0)
        start = across.shape[0] - 2 * half
        return self.flip(left, 2), self.other_copy(lax.dynamic_slice_in_dim(across, start + at[4], 2 * half, 0))

    def gather_core(self, at, *pieces):
        return [self.flip(jnp.concatenate([piece + at[4].astype(LOW) for piece in pieces], axis=0), 1)]

    def piece_list(self, early):
        blocks = [[(0, 0, None)]]
        if early:
            blocks.append([(0, 1, None)])
        blocks.append([(k, 0, 0) for k in (1, 2, 3)])
        blocks.append([(k, 1, 0) for k in ((1, 2, 3) if early else (0, 1, 2, 3))])
        blocks.append([(k, 0, 1) for k in (1, 2, 3)])
        blocks.append([(k, 1, 1) for k in ((1,) if early else (0, 1))])
        blocks.append([(k, 1, 1) for k in (2, 3)])
        main = len(blocks) - 2
        out, first = [], 0
        for core in (0, 1):
            for piece, content in enumerate(blocks):
                if core == 0 or piece in (0, main):
                    first = 0
                for dz, dx, dy in content:
                    size = 2 if dy is None else 1
                    at_piece = piece if core == 0 else len(blocks) + (piece >= main)
                    out.append((at_piece, first, size, dz, dx, core, dy))
                    first += size
        return out


    def part(self, at, mine, got, group, first=0, count=4):
        start = GROUPS.index(group) * 4 + first
        stop = start + count
        return mine[start:stop].astype(F32) + got[start:stop].astype(F32) + at[4].astype(F32)

    def scatter_corner(self, at, mine, got):
        return (
            self.flip(self.part(at, mine, got, CORNER, 0, 2).astype(LOW), 2),
            self.other_copy(self.part(at, mine, got, CORNER, 2, 2).astype(LOW)),
        )

    def scatter_xy(self, at, mine, got, corner_a, corner_b):
        other = jnp.concatenate(
            [self.part(at, mine, got, OTHER, 0, 2) + corner_a.astype(F32), self.part(at, mine, got, OTHER, 2, 2)], axis=0
        ).astype(LOW)
        across = jnp.concatenate(
            [self.part(at, mine, got, ACROSS, 0, 2), self.part(at, mine, got, ACROSS, 2, 2) + corner_b.astype(F32)], axis=0
        ).astype(LOW)
        return self.flip(across, 2), self.other_copy(other)

    def scatter_z(self, at, mine, got, across, other):
        own = self.part(at, mine, got, OWN) + across.astype(F32) + other.astype(F32)
        low = own.astype(LOW)
        return [own[0]] + [self.flip(low[k], 4 * k) for k in (1, 2, 3)]

    def scatter_end(self, at, parts):
        total = parts[0] + at[4].astype(F32)
        for value in parts[1:]:
            total = total + value.astype(F32)
        total = total.astype(LOW)
        away = self.other_copy(total)
        low = at[3] == 0
        return jnp.where(low, total, away).astype(F32), jnp.where(low, away, total).astype(F32)


def place():
    shard = lax.axis_index("fsdp")
    return jnp.stack(
        [shard // 4, (shard // 2) % 2, shard % 2, lax.axis_index("rep"), shard * 0]
    ).astype(jnp.int32)


AT = jax.ShapeDtypeStruct((5,), jnp.int32)
AT_SPEC = pl.BlockSpec(memory_space=pltpu.SMEM)


def hand_on(at, at_ref):
    for index in range(5):
        at_ref[index] = at[index]


def load_copies(plan, at, pieces, target, sem, rows, early):
    if len(pieces) == 1:
        return [pltpu.make_async_copy(pieces[0], target, sem)]
    half = rows // plan.shards // 2
    copies = []
    for piece, first, count, dz, dx, dc, dy in plan.piece_list(early):
        shard = (at[0] ^ dz) * 4 + (at[1] ^ dx) * 2 + (at[2] ^ dc)
        row = shard * 2 * half
        if dy is not None:
            row = row + (at[3] ^ dy) * half
        size = count * half
        copies.append(
            pltpu.make_async_copy(
                pieces[piece].at[pl.ds(first * half, size)], target.at[pl.ds(pl.multiple_of(row, half), size)], sem
            )
        )
    return copies


def fetch(plan, at, groups, sems):
    for index in range(len(groups)):
        for copy in load_copies(plan, at, *groups[index][:2], sems.at[index], *groups[index][2:]):
            copy.start()


def wait_for(plan, at, groups, sems, index):
    for copy in load_copies(plan, at, *groups[index][:2], sems.at[index], *groups[index][2:]):
        copy.wait()


def first_step(action):
    pl.when(pl.program_id(0) == 0)(action)


def project_kernel(plan, count, at, rows_ref, *refs):
    pieces, (out_ref, turned_ref, at_ref, weight, bias, sems) = refs[:count], refs[count:]
    depth = weight.shape[0]

    def load():
        hand_on(at, at_ref)
        groups = [(pieces, weight, weight.shape[0], True)]
        fetch(plan, at, groups, sems)
        wait_for(plan, at, groups, sems, 0)
        bias[...] = weight[:, 3 * depth :].astype(F32).T[:8]

    turned_ref[...] = rows_ref[...].T
    first_step(load)
    for block, row in ((0, 0), (1, None), (2, 1)):
        span = slice(block * depth, (block + 1) * depth)
        result = nn(rows_ref[...], weight[:, span])
        if row is not None:
            result = result + bias[row : row + 1]
        out_ref[:, span] = result.astype(LOW)


def project(plan, at, rows, pieces, depth, width, tile=256, after=()):
    count = len(pieces)
    height = rows.shape[0]
    return pl.pallas_call(
        later(functools.partial(project_kernel, plan, count), 1, after),
        out_shape=(jax.ShapeDtypeStruct((height, width), LOW), jax.ShapeDtypeStruct((depth, height), LOW), AT),
        grid_spec=pltpu.PrefetchScalarGridSpec(
            num_scalar_prefetch=1,
            grid=(height // tile,),
            in_specs=[ANY] * len(after)
            + [
                pl.BlockSpec((tile, depth), lambda i, at: (i, 0)),
            ]
            + [ANY] * count,
            out_specs=(
                pl.BlockSpec((tile, width), lambda i, at: (i, 0)),
                pl.BlockSpec((depth, tile), lambda i, at: (0, i)),
                AT_SPEC,
            ),
            scratch_shapes=[
                pltpu.VMEM((depth, width + EXTRA), LOW),
                pltpu.VMEM((8, depth), F32),
                pltpu.SemaphoreType.DMA((1,)),
            ],
        ),
        compiler_params=params(),
        cost_estimate=cost(2 * height * depth * width),
    )(at, *after, rows, *pieces)


def slot_rows(lengths_ref, block, row_count):
    along = lax.broadcasted_iota(jnp.int32, (1, row_count), 1)
    down = lax.broadcasted_iota(jnp.int32, (row_count, 1), 0)
    bound, lane_slot, row_slot = 0, jnp.zeros_like(along), jnp.zeros_like(down)
    for slot in range(SLOTS):
        bound = bound + lengths_ref[block, slot]
        lane_slot = lane_slot + (along >= bound).astype(jnp.int32)
        row_slot = row_slot + (down >= bound).astype(jnp.int32)
    return lane_slot, row_slot


def query_rows(lane_slot):
    line = lax.broadcasted_iota(jnp.int32, (8, lane_slot.shape[1]), 0)
    return jnp.where(line == lane_slot, -BIG, 0.0)


def key_columns(row_slot, offset):
    column = lax.broadcasted_iota(jnp.int32, (row_slot.shape[0], 128), 1) - offset
    barred = (column >= 0) & (column <= SLOTS) & ((column != row_slot) | (row_slot == SLOTS))
    return jnp.where(barred, 1.0, 0.0).astype(LOW)


def attend_kernel(lengths_ref, at, q_ref, k_ref, v_ref, out_ref, turned_ref, log_ref, at_ref):
    hand_on(at, at_ref)
    block = pl.program_id(0) // (H // 2)
    row_count = q_ref.shape[0]
    lane_slot, row_slot = slot_rows(lengths_ref, block, row_count)
    inside = lane_slot < SLOTS
    lane = lax.broadcasted_iota(jnp.int32, (row_count, 128), 1)
    barred = query_rows(lane_slot).astype(LOW)
    padded = jnp.concatenate([barred, jnp.zeros((HD - 8, row_count), LOW)], axis=0)
    q_turned = (q_ref[...].astype(F32) * SCALE).T.astype(LOW)
    v_turned = v_ref[...].astype(F32).T
    v_low = v_turned.astype(LOW)
    ones = jnp.ones((16, row_count), LOW)
    results = []
    for head in range(2):
        own = (lane < HD) if head == 0 else (lane >= HD)
        keyed = jnp.where(own, k_ref[...], key_columns(row_slot, HD * (1 - head)))
        half = q_turned[head * HD : (head + 1) * HD]
        query = jnp.concatenate([half, padded] if head == 0 else [padded, half], axis=0)
        scores = nn(keyed, query)
        highest = jnp.max(scores, axis=0, keepdims=True)
        weights = jnp.exp(scores - highest)
        low = weights.astype(LOW)
        values = jnp.concatenate([v_low[head * HD : (head + 1) * HD], ones], axis=0)
        mixed = nn(values, low)
        total = mixed[HD : HD + 1]
        result = mixed[:HD] / total
        results.append(jnp.where(inside, result, v_turned[head * HD : (head + 1) * HD]))
        log_ref[0, head : head + 1] = jnp.where(inside, highest + jnp.log(total), BIG)
    turned = jnp.concatenate(results, axis=0)
    turned_ref[...] = turned.astype(LOW)
    out_ref[...] = turned.T.astype(LOW)


def attend(at, lengths, projected, after=()):
    rows = projected.shape[0]
    blocks, pairs = rows // CAP, H // 2
    width = H * HD

    def column(part):
        return pl.BlockSpec((CAP, 128), lambda i, n, at: (i // pairs, part * pairs + i % pairs))

    return pl.pallas_call(
        later(attend_kernel, 2, after),
        out_shape=(
            jax.ShapeDtypeStruct((rows, width), LOW),
            jax.ShapeDtypeStruct((width, rows), LOW),
            jax.ShapeDtypeStruct((blocks * pairs, 8, CAP), F32),
            AT,
        ),
        grid_spec=pltpu.PrefetchScalarGridSpec(
            num_scalar_prefetch=2,
            grid=(blocks * pairs,),
            in_specs=[ANY] * len(after) + [column(0), column(1), column(2)],
            out_specs=(
                column(0),
                pl.BlockSpec((128, CAP), lambda i, n, at: (i % pairs, i // pairs)),
                pl.BlockSpec((1, 8, CAP), lambda i, n, at: (i, 0, 0)),
                AT_SPEC,
            ),
        ),
        compiler_params=params(),
        cost_estimate=cost(4 * rows * CAP * width, 12),
    )(lengths, at, *after, projected, projected, projected)


def three(value):
    first = value.astype(LOW).astype(F32)
    rest = value - first
    second = rest.astype(LOW).astype(F32)
    return first, second, rest - second


def attend_back_kernel(lengths_ref, at, q_ref, k_ref, v_ref, att_ref, grad_ref, log_ref, dq_ref, dk_ref, dv_ref, sums_ref, at_ref):
    hand_on(at, at_ref)
    block, pair = pl.program_id(0) // (H // 2), pl.program_id(0) % (H // 2)
    row_count = q_ref.shape[0]
    lane_slot, row_slot = slot_rows(lengths_ref, block, row_count)
    outside = lane_slot >= SLOTS
    lane = lax.broadcasted_iota(jnp.int32, (row_count, 128), 1)
    barred = query_rows(lane_slot)
    q_scaled = (q_ref[...].astype(F32) * SCALE)
    q_turned = q_scaled.T.astype(LOW)
    k_scaled = k_ref[...].astype(F32) * SCALE
    k_turned = k_scaled.T.astype(LOW)
    grad_wide = grad_ref[...].astype(F32).T
    grad_turned = grad_wide
    mixed = grad_turned * att_ref[...].astype(F32)
    grad_turned = grad_turned.astype(LOW)
    line = lax.broadcasted_iota(jnp.int32, (8, row_count), 0)
    none = jnp.zeros((HD - 16, row_count), F32)

    def lines(value):
        first, second, third = three(value)
        return jnp.where(
            line == 0, -first, jnp.where(line == 1, -second, jnp.where(line == 2, -third, 0.0))
        )

    dqs, dks, dvs = [], [], []
    for head in range(2):
        own = (lane < HD) if head == 0 else (lane >= HD)
        start = HD * (1 - head)
        unit = (lane >= start + 8) & (lane < start + 11)
        keyed = jnp.where(own, k_ref[...], jnp.where(unit, jnp.ones((), LOW), key_columns(row_slot, start)))
        valued = jnp.where(own, v_ref[...], jnp.where(unit, jnp.ones((), LOW), jnp.zeros((), LOW)))
        extra = jnp.concatenate([barred, lines(log_ref[0, head : head + 1]), none], axis=0).astype(LOW)
        half = slice(head * HD, (head + 1) * HD)
        query = jnp.concatenate([q_turned[half], extra] if head == 0 else [extra, q_turned[half]], axis=0)
        weights = jnp.exp(nn(keyed, query))
        inner = jnp.sum(mixed[half], axis=0, keepdims=True)
        extra = jnp.concatenate([jnp.zeros_like(barred), lines(inner), none], axis=0).astype(LOW)
        grad = jnp.concatenate([grad_turned[half], extra] if head == 0 else [extra, grad_turned[half]], axis=0)
        moved = (weights * nn(valued, grad)).astype(LOW)
        dvs.append(nt(grad_turned[half], weights.astype(LOW)))
        dks.append(nt(q_turned[half], moved))
        dqs.append(nn(k_turned[half], moved))
    dq = jnp.concatenate(dqs, axis=0).T.astype(LOW)
    dq_ref[...] = dq
    dk_ref[...] = jnp.concatenate(dks, axis=0).T.astype(LOW)
    dv = jnp.concatenate(dvs, axis=0)
    dv = jnp.where(outside, dv + grad_wide, dv).T.astype(LOW)
    dv_ref[...] = dv

    @first_step
    def _():
        sums_ref[...] = jnp.zeros_like(sums_ref)

    span = pl.ds(pl.multiple_of(pair * 128, 128), 128)
    sums_ref[0:1, span] += jnp.sum(dq.astype(F32), axis=0, keepdims=True)
    sums_ref[1:2, span] += jnp.sum(dv.astype(F32), axis=0, keepdims=True)


def attend_back(at, lengths, projected, turned, grad_attended, logs, after=()):
    rows = projected.shape[0]
    blocks, pairs = rows // CAP, H // 2
    width = H * HD

    def column(part):
        return pl.BlockSpec((CAP, 128), lambda i, n, at: (i // pairs, part * pairs + i % pairs))

    return pl.pallas_call(
        later(attend_back_kernel, 2, after),
        out_shape=(jax.ShapeDtypeStruct((rows, width), LOW),) * 3 + (jax.ShapeDtypeStruct((8, width), F32), AT),
        grid_spec=pltpu.PrefetchScalarGridSpec(
            num_scalar_prefetch=2,
            grid=(blocks * pairs,),
            in_specs=[ANY] * len(after)
            + [
                column(0), column(1), column(2),
                pl.BlockSpec((128, CAP), lambda i, n, at: (i % pairs, i // pairs)),
                column(0),
                pl.BlockSpec((1, 8, CAP), lambda i, n, at: (i, 0, 0)),
            ],
            out_specs=(column(0),) * 3 + (pl.BlockSpec((8, width), lambda i, n, at: (0, 0)), AT_SPEC),
        ),
        compiler_params=params(),
        cost_estimate=cost(10 * rows * CAP * width, 5),
    )(lengths, at, *after, projected, projected, projected, turned, grad_attended, logs)


def norm(values):
    centre = jnp.mean(values, axis=-1, keepdims=True)
    centred = values - centre
    scale = lax.rsqrt(jnp.mean(centred * centred, axis=-1, keepdims=True) + EPSILON)
    return centred * scale, scale


def norm_back(grad, normal, scale):
    return scale * (
        grad
        - jnp.mean(grad, axis=-1, keepdims=True)
        - normal * jnp.mean(grad * normal, axis=-1, keepdims=True)
    )


ROOT_HALF = 0.7071067811865476
ROOT_TAU = 0.3989422804014327


def up_kernel(plan, chunk, at, rows_ref, att_ref, *refs):
    pieces = refs[:-11]
    (
        active_ref, slope_ref, normal_ref, scale_ref, first_ref, turned_ref, small_ref, at_ref, w_wide, wide_ref, sems,
    ) = refs[-11:]
    depth = w_wide.shape[0]
    hidden = w_wide.shape[1] - depth - EXTRA
    groups = [(pieces, w_wide, depth, False)]

    def load():
        hand_on(at, at_ref)
        fetch(plan, at, groups, sems)
        wait_for(plan, at, groups, sems, 0)
        table = w_wide[:, hidden + depth :].astype(F32).T
        small_ref[...] = table[:8]
        part = depth // plan.shards
        for shard in range(plan.shards):
            for line in range(hidden // depth):
                start = (shard * (hidden // depth) + line) * part
                wide_ref[0:1, start : start + part] = table[8 + line : 9 + line, shard * part : (shard + 1) * part]

    first_step(load)

    def small(index):
        return small_ref[index : index + 1]

    residual = rows_ref[...].astype(F32) + nn(att_ref[...], w_wide[:, hidden : hidden + depth]) + small(0)
    normal, scale = norm(residual)
    normal_ref[...] = normal.astype(LOW)
    scale_ref[...] = jnp.broadcast_to(scale, scale_ref.shape)
    first = normal * small(2) + small(3)
    first_ref[...] = first
    low = first.astype(LOW)
    turned_ref[...] = low.T
    for start in range(0, hidden, chunk):
        span = slice(start, start + chunk)
        wide = nn(low, w_wide[:, span]) + wide_ref[0:1, span]
        cumulative = 0.5 * (1.0 + lax.erf(wide * ROOT_HALF))
        active_ref[:, span] = (wide * cumulative).astype(LOW)
        slope_ref[:, span] = (cumulative + wide * (ROOT_TAU * jnp.exp(-0.5 * wide * wide))).astype(LOW)


def tiled(tile, width):
    return pl.BlockSpec((tile, width), lambda i, at: (i, 0))


def turned_tile(tile, width):
    return pl.BlockSpec((width, tile), lambda i, at: (0, i))


def whole_block(height, width):
    return pl.BlockSpec((height, width), lambda i, at: (0, 0))


def up(plan, at, rows, attended, hidden, pieces, tile=256, chunk=1024, after=()):
    height, depth = rows.shape
    return pl.pallas_call(
        later(functools.partial(up_kernel, plan, chunk), 1, after),
        out_shape=(
            jax.ShapeDtypeStruct((height, hidden), LOW),
            jax.ShapeDtypeStruct((height, hidden), LOW),
            jax.ShapeDtypeStruct((height, depth), LOW),
            jax.ShapeDtypeStruct((height, 128), F32),
            jax.ShapeDtypeStruct((height, depth), F32),
            jax.ShapeDtypeStruct((depth, height), LOW),
            jax.ShapeDtypeStruct((8, depth), F32),
            AT,
        ),
        grid_spec=pltpu.PrefetchScalarGridSpec(
            num_scalar_prefetch=1,
            grid=(height // tile,),
            in_specs=[ANY] * len(after) + [tiled(tile, depth), tiled(tile, depth)] + [ANY] * len(pieces),
            out_specs=(
                tiled(tile, hidden), tiled(tile, hidden), tiled(tile, depth), tiled(tile, 128),
                tiled(tile, depth), turned_tile(tile, depth), whole_block(8, depth), AT_SPEC,
            ),
            scratch_shapes=[
                pltpu.VMEM((depth, hidden + depth + EXTRA), LOW),
                pltpu.VMEM((8, hidden), F32),
                pltpu.SemaphoreType.DMA((1,)),
            ],
        ),
        compiler_params=params(),
        cost_estimate=cost(2 * height * depth * (depth + hidden)),
    )(at, *after, rows, attended, *pieces)


def over_kernel(plan, chunk, at, first_ref, active_ref, cot_ref, small_ref, *refs):
    pieces = refs[:-6]
    result_ref, second_ref, sums_ref, at_ref, w_contract, sems = refs[-6:]
    hidden = w_contract.shape[0]
    groups = [(pieces, w_contract, hidden, False)]

    def load():
        hand_on(at, at_ref)
        fetch(plan, at, groups, sems)
        sums_ref[...] = jnp.zeros_like(sums_ref)
        wait_for(plan, at, groups, sems, 0)

    first_step(load)

    def small(index):
        return small_ref[index : index + 1].astype(F32)

    def add(index, value):
        sums_ref[index : index + 1] += jnp.sum(value, axis=0, keepdims=True)

    normal, scale = norm(first_ref[...] + small(1) + nn(active_ref[...], w_contract[...]))
    result_ref[...] = (normal * small(4) + small(5)).astype(LOW)
    cot = cot_ref[...].astype(F32)
    add(4, cot * normal)
    add(5, cot)
    second = norm_back(cot * small(4), normal, scale).astype(LOW)
    second_ref[...] = second
    add(1, second.astype(F32))


def over(plan, at, first, active, cot, small, pieces, tile=256, chunk=1024, after=()):
    height, depth = first.shape
    hidden = active.shape[1]
    return pl.pallas_call(
        later(functools.partial(over_kernel, plan, chunk), 1, after),
        out_shape=(
            jax.ShapeDtypeStruct((height, depth), LOW),
            jax.ShapeDtypeStruct((height, depth), LOW),
            jax.ShapeDtypeStruct((8, depth), F32),
            AT,
        ),
        grid_spec=pltpu.PrefetchScalarGridSpec(
            num_scalar_prefetch=1,
            grid=(height // tile,),
            in_specs=[ANY] * len(after)
            + [tiled(tile, depth), tiled(tile, hidden), tiled(tile, depth), whole_block(8, depth)]
            + [ANY] * len(pieces),
            out_specs=(
                tiled(tile, depth), tiled(tile, depth), whole_block(8, depth), AT_SPEC,
            ),
            scratch_shapes=[pltpu.VMEM((hidden, depth), LOW), pltpu.SemaphoreType.DMA((1,))],
        ),
        compiler_params=params(),
        cost_estimate=cost(2 * height * depth * hidden),
    )(at, *after, first, active, cot, small, *pieces)


def down_kernel(plan, counts, chunk, at, second_ref, slope_ref, normal_ref, scale_ref, small_ref, *refs):
    first_count, second_count = counts
    wide_pieces, contract_pieces = refs[:first_count], refs[first_count : first_count + second_count]
    expanded_ref, branch_ref, grad_att_ref, sums_ref, wide_sums_ref, at_ref, w_wide, w_contract, sems = refs[
        first_count + second_count :
    ]
    hidden, depth = w_contract.shape

    groups = [(contract_pieces, w_contract, hidden, False), (wide_pieces, w_wide, depth, False)]

    def load():
        hand_on(at, at_ref)
        fetch(plan, at, groups, sems)
        sums_ref[...] = jnp.zeros_like(sums_ref)
        wide_sums_ref[...] = jnp.zeros_like(wide_sums_ref)
        wait_for(plan, at, groups, sems, 0)

    first_step(load)

    def add(index, value):
        sums_ref[index : index + 1] += jnp.sum(value, axis=0, keepdims=True)

    second = second_ref[...]
    total = second.astype(F32)
    for start in range(0, hidden, chunk):
        span = slice(start, start + chunk)
        grad = (nt(second, w_contract[span]) * slope_ref[:, span].astype(F32)).astype(LOW)
        expanded_ref[:, span] = grad
        wide_sums_ref[0:1, span] += jnp.sum(grad.astype(F32), axis=0, keepdims=True)
        if start == 0:
            first_step(lambda: wait_for(plan, at, groups, sems, 1))
        total = total + nt(grad, w_wide[:, span])
    normal = normal_ref[...].astype(F32)
    add(2, total * normal)
    add(3, total)
    branch = norm_back(total * small_ref[2:3].astype(F32), normal, scale_ref[:, 0:1]).astype(LOW)
    branch_ref[...] = branch
    add(0, branch.astype(F32))
    grad_att_ref[...] = nt(branch, w_wide[:, hidden : hidden + depth]).astype(LOW)


def down(plan, at, second, slope, normal, scale, small, wide_pieces, contract_pieces, tile=256, chunk=1024, after=()):
    height, depth = second.shape
    hidden = slope.shape[1]

    def tiled(width):
        return pl.BlockSpec((tile, width), lambda i, at: (i, 0))

    def whole(height, width):
        return pl.BlockSpec((height, width), lambda i, at: (0, 0))

    return pl.pallas_call(
        later(functools.partial(down_kernel, plan, (len(wide_pieces), len(contract_pieces)), chunk), 1, after),
        out_shape=(
            jax.ShapeDtypeStruct((height, hidden), LOW),
            jax.ShapeDtypeStruct((height, depth), LOW),
            jax.ShapeDtypeStruct((height, depth), LOW),
            jax.ShapeDtypeStruct((8, depth), F32),
            jax.ShapeDtypeStruct((8, hidden), F32),
            AT,
        ),
        grid_spec=pltpu.PrefetchScalarGridSpec(
            num_scalar_prefetch=1,
            grid=(height // tile,),
            in_specs=[ANY] * len(after)
            + [tiled(depth), tiled(hidden), tiled(depth), tiled(128), whole(8, depth)]
            + [ANY] * (len(wide_pieces) + len(contract_pieces)),
            out_specs=(tiled(hidden), tiled(depth), tiled(depth), whole(8, depth), whole(8, hidden), AT_SPEC),
            scratch_shapes=[
                pltpu.VMEM((depth, hidden + depth + EXTRA), LOW),
                pltpu.VMEM((hidden, depth), LOW),
                pltpu.SemaphoreType.DMA((2,)),
            ],
        ),
        compiler_params=params(),
        cost_estimate=cost(2 * height * depth * (depth + 2 * hidden)),
    )(at, *after, second, slope, normal, scale, small, *wide_pieces, *contract_pieces)


def source(at, flip, group, k):
    shard = (at[0] ^ k) * 4 + (at[1] ^ (group % 2)) * 2 + (at[2] ^ flip)
    return shard * 2 + (at[3] ^ (group // 2))


def outer_tall_kernel(at, left, right, out, at_ref):
    hand_on(at, at_ref)
    out[...] = tn(left[...], right[...]).astype(LOW)


def outer_tall(at, left, right, tile=512, after=()):
    height, rows = left.shape
    width = right.shape[1]
    return pl.pallas_call(
        later(outer_tall_kernel, 1, after),
        out_shape=(jax.ShapeDtypeStruct((rows, width), LOW), AT),
        grid_spec=pltpu.PrefetchScalarGridSpec(
            num_scalar_prefetch=1,
            grid=(rows // tile,),
            in_specs=[ANY] * len(after)
            + [pl.BlockSpec((height, tile), lambda i, at: (0, i)), whole_block(height, width)],
            out_specs=(tiled(tile, width), AT_SPEC),
        ),
        compiler_params=params(),
        cost_estimate=cost(2 * height * rows * width),
    )(at, *after, left, right)


def outer_row_kernel(count, tile, at, turned, extra, *refs):
    rights, (out, at_ref) = refs[:count], refs[count:]
    step = pl.program_id(0)
    total = out.shape[1] - EXTRA
    steps = total // tile // count
    for place in range(count * steps):

        @pl.when(step == place)
        def _(place=place):
            out[:, place * tile : (place + 1) * tile] = nn(turned[...], rights[place // steps][...]).astype(LOW)

    @first_step
    def _():
        hand_on(at, at_ref)
        lines = jnp.zeros((EXTRA - extra.shape[0], extra.shape[1]), F32)
        out[:, total:] = jnp.concatenate([extra[...], lines], axis=0).T.astype(LOW)


def outer_row(at, turned, rights, extra, tile=512, after=()):
    rows, height = turned.shape
    steps = rights[0].shape[1] // tile
    count = len(rights)
    width = count * steps * tile

    def column(index):
        return pl.BlockSpec((height, tile), lambda i, at: (0, jnp.clip(i - index * steps, 0, steps - 1)))

    return pl.pallas_call(
        later(functools.partial(outer_row_kernel, count, tile), 1, after),
        out_shape=(jax.ShapeDtypeStruct((rows, width + EXTRA), LOW), AT),
        grid_spec=pltpu.PrefetchScalarGridSpec(
            num_scalar_prefetch=1,
            grid=(count * steps,),
            in_specs=[ANY] * len(after)
            + [whole_block(rows, height), whole_block(*extra.shape)]
            + [column(index) for index in range(count)],
            out_specs=(whole_block(rows, width + EXTRA), AT_SPEC),
        ),
        compiler_params=params(),
        cost_estimate=cost(2 * height * rows * width),
    )(at, *after, turned, extra, *rights)


def outer_wide_kernel(flip, owners, firsts, tile, extra, at, *refs):
    count = max(owners) + 1
    turned, rights = refs[:count], refs[count : count + len(owners)]
    if extra:
        extra_ref, out, at_ref, lines, held, sem = refs[-6:]
    else:
        out, at_ref, held, sem = refs[-4:]
    step = pl.program_id(0)
    half = held.shape[1] // 16

    def load():
        hand_on(at, at_ref)
        copies = []
        for index, ref in enumerate(turned):
            for group in range(4):
                for k in range(4):
                    row = pl.multiple_of(source(at, flip, group, k) * half, half)
                    copies.append(
                        pltpu.make_async_copy(
                            ref.at[pl.ds(row, half)], held.at[index, pl.ds((group * 4 + k) * half, half)], sem
                        )
                    )
        for copy in copies:
            copy.start()
        for copy in copies:
            copy.wait()

    first_step(load)
    if extra:
        @first_step
        def _():
            rest = jnp.zeros((EXTRA - extra_ref.shape[0], extra_ref.shape[1]), F32)
            lines[...] = jnp.concatenate([extra_ref[...], rest], axis=0).T.astype(LOW)
            for group in range(4):
                for k in range(4):
                    row = pl.multiple_of(source(at, flip, group, k) * half, half)
                    out[group * 4 + k, :, tile * firsts[-1] :] = lines[pl.ds(row, half), :]

    for index, owner in enumerate(owners):
        if extra:
            for place in range(firsts[index], firsts[index + 1]):

                @pl.when(step == place)
                def _(index=index, owner=owner, place=place):
                    result = nn(held[owner], rights[index][...]).astype(LOW)
                    out[:, :, place * tile : (place + 1) * tile] = result.reshape(16, half, tile)

            continue

        @pl.when((step >= firsts[index]) & (step < firsts[index + 1]))
        def _(index=index, owner=owner):
            result = nn(held[owner], rights[index][...]).astype(LOW)
            out[...] = result.reshape(out.shape)


def outer_wide(at, turned, rights, owners, flip, tile=1024, extra=None, after=()):
    rows, height = turned[0].shape
    half = rows // 32
    counts = [right.shape[1] // tile for right in rights]
    firsts = [sum(counts[:i]) for i in range(len(counts) + 1)]
    width = tile * firsts[-1]
    more = [] if extra is None else [extra]
    wide = width + EXTRA * len(more)
    block = pl.BlockSpec((16, half, tile), lambda i, at: (0, 0, i))
    if more:
        block = pl.BlockSpec((16, half, wide), lambda i, at: (0, 0, 0))

    def column(index):
        return pl.BlockSpec((height, tile), lambda i, at: (0, jnp.clip(i - firsts[index], 0, counts[index] - 1)))

    return pl.pallas_call(
        later(functools.partial(outer_wide_kernel, flip, tuple(owners), tuple(firsts), tile, bool(more)), 1, after),
        out_shape=(jax.ShapeDtypeStruct((16, half, wide), LOW), AT),
        grid_spec=pltpu.PrefetchScalarGridSpec(
            num_scalar_prefetch=1,
            grid=(firsts[-1],),
            in_specs=[ANY] * len(after)
            + [ANY] * len(turned)
            + [column(index) for index in range(len(rights))]
            + [whole_block(*line.shape) for line in more],
            out_specs=(block, AT_SPEC),
            scratch_shapes=[pltpu.VMEM((rows, EXTRA), LOW) for line in more]
            + [pltpu.VMEM((len(turned), rows // 2, height), LOW), pltpu.SemaphoreType.DMA],
        ),
        compiler_params=params(),
        cost_estimate=cost(height * rows * width),
    )(at, *after, *turned, *rights, *more)


def owned_sum(whole):
    return lax.psum_scatter(whole, "fsdp", scatter_dimension=0, tiled=True)


def copies_sum(plan, at, owned):
    if plan.copies == 2:
        owned = owned + at[4].astype(LOW)
        return owned.astype(F32) + plan.other_copy(owned).astype(F32)
    return lax.psum(owned, "rep").astype(F32)


def back_kernel(plan, count, at, branch_ref, dq_ref, dk_ref, dv_ref, *refs):
    pieces, (out_ref, at_ref, weight, sems) = refs[:count], refs[count:]
    width = dq_ref.shape[1]

    def load():
        hand_on(at, at_ref)
        groups = [(pieces, weight, weight.shape[0], True)]
        fetch(plan, at, groups, sems)
        wait_for(plan, at, groups, sems, 0)

    first_step(load)

    total = branch_ref[...].astype(F32)
    for index, ref in enumerate((dq_ref, dk_ref, dv_ref)):
        total = total + nt(ref[...], weight[:, index * width : (index + 1) * width])
    out_ref[...] = total.astype(LOW)


def back(plan, at, branch, dq, dk, dv, pieces, tile=256, after=()):
    count = len(pieces)
    height, depth = branch.shape
    width = dq.shape[1]
    tiled = pl.BlockSpec((tile, depth), lambda i, at: (i, 0))
    return pl.pallas_call(
        later(functools.partial(back_kernel, plan, count), 1, after),
        out_shape=(jax.ShapeDtypeStruct((height, depth), LOW), AT),
        grid_spec=pltpu.PrefetchScalarGridSpec(
            num_scalar_prefetch=1,
            grid=(height // tile,),
            in_specs=[ANY] * len(after)
            + [tiled] * 4 + [ANY] * count,
            out_specs=(tiled, AT_SPEC),
            scratch_shapes=[pltpu.VMEM((depth, 3 * width + EXTRA), LOW), pltpu.SemaphoreType.DMA((1,))],
        ),
        compiler_params=params(),
        cost_estimate=cost(6 * height * depth * width),
    )(at, *after, branch, dq, dk, dv, *pieces)


def body(
    tokens, seq_lengths, out_cotangent, project_in, project_out, expand, contract,
    query_bias, value_bias, out_bias, expand_bias, contract_bias,
    first_gain, first_shift, second_gain, second_shift,
    *, shards, copies,
):
    plan = Plan(shards, copies)
    at = place()
    depth = tokens.shape[1]
    hidden = expand.shape[1]
    part, wide_part = query_bias.shape[0], expand_bias.shape[0]

    def columns(*vectors):
        table = jnp.stack([vector for vector in vectors], axis=1)
        return jnp.pad(table, ((0, 0), (0, EXTRA - len(vectors))))

    zero = jnp.zeros_like(query_bias)
    in_shard = jnp.concatenate([project_in, columns(query_bias, value_bias)], axis=1)
    wide_bias = tuple(expand_bias[i * part : (i + 1) * part] for i in range(wide_part // part))
    small = (out_bias, contract_bias, first_gain, first_shift, second_gain, second_shift, zero, zero)
    wide_shard = jnp.concatenate([expand, project_out, columns(*small, *wide_bias)], axis=1)
    width = project_in.shape[1]
    if plan.split:
        in_beside, in_parts = plan.gather_z(at, in_shard, True)
        in_far, in_across, in_other = plan.gather_xy(at, in_shard, in_parts, True)
        unused, wide_parts = plan.gather_z(pinned(at, in_parts[2]), wide_shard)
        in_corners = plan.gather_corner(at, in_shard, in_across, in_other, True)
        in_main = (in_shard, in_beside, in_far, in_across, in_other)
        at_wide = pinned(at, *wide_parts)
        in_cores = plan.gather_core(at, *in_main) + plan.gather_core(at_wide, *in_corners)
        in_pieces = list(in_main + in_corners) + in_cores
        at_core = pinned(at_wide, *in_corners)
        wide_far, wide_across, wide_other = plan.gather_xy(at_core, wide_shard, wide_parts)
        contract_pieces = [lax.all_gather(contract + pinned(at_core, wide_across, wide_other)[4].astype(LOW), "fsdp", axis=0, tiled=True)]
        wide_corners = plan.gather_corner(at_core, wide_shard, wide_across, wide_other)
    else:
        in_pieces, wide_pieces, contract_pieces = (
            [lax.all_gather(shard, "fsdp", axis=0, tiled=True)] for shard in (in_shard, wide_shard, contract)
        )
    first_after = [wide_across, wide_other] if plan.split else []
    projected, tokens_turned, at = project(plan, at, tokens, in_pieces, depth, width, after=first_after)
    if plan.split:
        wide_main = (wide_shard, wide_far, wide_across, wide_other)
        attended, attended_turned, logs, at = attend(at, seq_lengths, projected, after=wide_corners)
        wide_pieces = list(wide_main + wide_corners)
        wide_pieces += plan.gather_core(at, *wide_main) + plan.gather_core(at, *wide_corners)
    else:
        attended, attended_turned, logs, at = attend(at, seq_lengths, projected)
    active, slope, normal, scale, first, first_turned, table, at = up(plan, at, tokens, attended, hidden, wide_pieces)
    result, second, sums, at = over(plan, at, first, active, out_cotangent, table, contract_pieces)
    whole, at = outer_tall(at, active, second)
    contract_owned = owned_sum(whole)
    grad_expanded, branch, grad_attended, more_sums, wide_sums, at = down(
        plan, at, second, slope, normal, scale, table, wide_pieces, contract_pieces
    )
    lines = wide_sums[0].reshape(shards, wide_part // part, part).transpose(1, 0, 2).reshape(-1, depth)
    lines = jnp.concatenate([sums[:6] + more_sums[:6], lines], axis=0)
    lines = jnp.pad(lines, ((0, 14 - lines.shape[0]), (0, 0)))
    if plan.split:
        turned, rights, owners = (first_turned, attended_turned), (grad_expanded, branch), (0, 1)
        theirs, at = outer_wide(at, turned, rights, owners, 1)
        e_got = plan.flip(theirs, 1)
        e_mine, at = outer_wide(at, turned, rights, owners, 0)
        e_corners = plan.scatter_corner(at, e_mine, e_got)
        dq, dk, dv, back_sums, at = attend_back(at, seq_lengths, projected, attended_turned, grad_attended, logs)
        e_across, e_other = plan.scatter_xy(at, e_mine, e_got, *e_corners)
        extra = jnp.concatenate([back_sums[:2], lines], axis=0)
        turned, rights, owners = (tokens_turned,), (dq, dk, dv), (0, 0, 0)
        theirs, at = outer_wide(at, turned, rights, owners, 1, extra=extra, after=[*e_corners, contract_owned])
        contract_sum = copies_sum(plan, at, contract_owned)
        i_got = plan.flip(theirs, 1)
        i_mine, at = outer_wide(at, turned, rights, owners, 0, extra=extra)
        e_parts = plan.scatter_z(at, e_mine, e_got, e_across, e_other)
        i_corners = plan.scatter_corner(at, i_mine, i_got)
        grad_tokens, at = back(plan, at, branch, dq, dk, dv, in_pieces, after=[i_got])
        i_across, i_other = plan.scatter_xy(at, i_mine, i_got, *i_corners)
        e_ends = plan.scatter_end(at, e_parts)
        i_parts = plan.scatter_z(at, i_mine, i_got, i_across, i_other)
        owned = jnp.concatenate(plan.scatter_end(at, i_parts), axis=0)
        grad_wide = jnp.concatenate(e_ends, axis=0)
        grad_expand, grad_project_out = grad_wide[:, :hidden], grad_wide[:, hidden:]
    else:
        none = jnp.zeros((8, depth), F32)
        whole, at = outer_row(at, first_turned, (grad_expanded,), none)
        grad_expand = copies_sum(plan, at, owned_sum(whole))[:, :hidden]
        whole, at = outer_row(at, attended_turned, (branch,), none)
        grad_project_out = copies_sum(plan, at, owned_sum(whole))[:, :depth]
        dq, dk, dv, back_sums, at = attend_back(at, seq_lengths, projected, attended_turned, grad_attended, logs)
        extra = jnp.concatenate([back_sums[:2], lines], axis=0)
        whole, at = outer_row(at, tokens_turned, (dq, dk, dv), extra)
        owned = copies_sum(plan, at, owned_sum(whole))
        contract_sum = copies_sum(plan, at, contract_owned)
        grad_tokens, at = back(plan, at, branch, dq, dk, dv, in_pieces)
    grad_contract = contract_sum
    grad_project_in = owned[:, :width]
    small = owned[:, width : width + 8 + wide_part // part].T
    grad_query, grad_value, grad_out, grad_down, gain_one, shift_one, gain_two, shift_two = (small[i] for i in range(8))
    grad_wide_bias = small[8:].reshape(-1)
    return (
        result, grad_tokens, grad_project_in, grad_project_out, grad_expand, grad_contract,
        grad_query, grad_value, grad_out, grad_wide_bias, grad_down,
        gain_one, shift_one, gain_two, shift_two,
    )


def solution(mesh):
    split, row, vector = P(("fsdp", "rep"), None), P("fsdp", None), P("fsdp")
    return jax.shard_map(
        functools.partial(body, shards=mesh.shape["fsdp"], copies=mesh.shape["rep"]),
        mesh=mesh,
        in_specs=(split,) * 3 + (row,) * 4 + (vector,) * 9,
        out_specs=(split,) * 2 + (row,) * 4 + (vector,) * 9,
        check_vma=False,
    )
```

```python
import functools

import jax
import jax.numpy as jnp
from jax import lax
from jax.experimental import pallas as pl
from jax.experimental.pallas import tpu as pltpu
from jax.sharding import PartitionSpec as P

H = 16
HD = 64
SLOTS = 4
CAP = 512
EPSILON = 1e-12
SCALE = 0.125
BIG = 1e30
PAIRS = 4
EXTRA = 128
HASTE = 1
LOW = jnp.bfloat16
F32 = jnp.float32
VMEM_LIMIT = 60 * 1024 * 1024
ANY = pl.BlockSpec(memory_space=pl.ANY)
OWN, ACROSS, OTHER, CORNER = (0, 0), (1, 0), (0, 1), (1, 1)
GROUPS = (OWN, ACROSS, OTHER, CORNER)


def params(limit=VMEM_LIMIT):
    return pltpu.CompilerParams(vmem_limit_bytes=limit, dimension_semantics=("arbitrary",))


def cost(flops, slow=2):
    return pl.CostEstimate(flops=slow * flops // HASTE, bytes_accessed=slow * flops // HASTE // 320, transcendentals=0)


def later(kernel, prefetch, after):
    def run(*refs):
        kernel(*refs[:prefetch], *refs[prefetch + len(after) :])

    return run


def dot(left, right, over):
    return lax.dot_general(left, right, ((over[:1], over[1:]), ((), ())), preferred_element_type=F32)


def nn(left, right):
    return dot(left, right, (1, 0))


def nt(left, right):
    return dot(left, right, (1, 1))


def tn(left, right):
    return dot(left, right, (0, 0))


def pinned(at, *values):
    for value in values:
        sample = jnp.clip(value[(0,) * value.ndim].astype(F32), -1.0, 1.0).astype(jnp.int32)
        at = at + jnp.minimum(jnp.abs(sample), 0)
    return at


class Plan:
    def __init__(self, shards, copies):
        self.shards, self.copies = shards, copies
        self.split = shards == 16 and copies == 2

    def flip(self, value, bits):
        return lax.ppermute(value, "fsdp", [(i, i ^ bits) for i in range(self.shards)])

    def other_copy(self, value):
        return lax.ppermute(value, "rep", [(0, 1), (1, 0)])


    def gather_z(self, at, shard, early=False):
        half = shard.shape[0] // 2
        own = lax.dynamic_slice_in_dim(shard, at[3] * half, half, 0)
        beside = self.flip(shard, 2) if early else None
        return beside, [self.flip(own, 4 * k) for k in (1, 2, 3)]

    def gather_xy(self, at, shard, far, early=False):
        half = shard.shape[0] // 2
        far = jnp.concatenate([part + at[4].astype(LOW) for part in far], axis=0)
        own = lax.dynamic_slice_in_dim(shard, at[3] * half, half, 0)
        across = far if early else jnp.concatenate([own, far], axis=0)
        return far, self.flip(across, 2), self.other_copy(far)

    def gather_corner(self, at, shard, across, other, early=False):
        half = shard.shape[0] // 2
        left = lax.dynamic_slice_in_dim(other, at[4], half, 0)
        if not early:
            left = jnp.concatenate([lax.dynamic_slice_in_dim(shard, (1 - at[3]) * half, half, 0), left], axis=0)
        start = across.shape[0] - 2 * half
        return self.flip(left, 2), self.other_copy(lax.dynamic_slice_in_dim(across, start + at[4], 2 * half, 0))

    def gather_core(self, at, *pieces):
        return [self.flip(jnp.concatenate([piece + at[4].astype(LOW) for piece in pieces], axis=0), 1)]

    def piece_list(self, early):
        blocks = [[(0, 0, None)]]
        if early:
            blocks.append([(0, 1, None)])
        blocks.append([(k, 0, 0) for k in (1, 2, 3)])
        blocks.append([(k, 1, 0) for k in ((1, 2, 3) if early else (0, 1, 2, 3))])
        blocks.append([(k, 0, 1) for k in (1, 2, 3)])
        blocks.append([(k, 1, 1) for k in ((1,) if early else (0, 1))])
        blocks.append([(k, 1, 1) for k in (2, 3)])
        main = len(blocks) - 2
        out, first = [], 0
        for core in (0, 1):
            for piece, content in enumerate(blocks):
                if core == 0 or piece in (0, main):
                    first = 0
                for dz, dx, dy in content:
                    size = 2 if dy is None else 1
                    at_piece = piece if core == 0 else len(blocks) + (piece >= main)
                    out.append((at_piece, first, size, dz, dx, core, dy))
                    first += size
        return out


    def part(self, at, mine, got, group, first=0, count=4):
        start = GROUPS.index(group) * 4 + first
        stop = start + count
        return mine[start:stop].astype(F32) + got[start:stop].astype(F32) + at[4].astype(F32)

    def scatter_corner(self, at, mine, got):
        return (
            self.flip(self.part(at, mine, got, CORNER, 0, 2).astype(LOW), 2),
            self.other_copy(self.part(at, mine, got, CORNER, 2, 2).astype(LOW)),
        )

    def scatter_xy(self, at, mine, got, corner_a, corner_b):
        other = jnp.concatenate(
            [self.part(at, mine, got, OTHER, 0, 2) + corner_a.astype(F32), self.part(at, mine, got, OTHER, 2, 2)], axis=0
        ).astype(LOW)
        across = jnp.concatenate(
            [self.part(at, mine, got, ACROSS, 0, 2), self.part(at, mine, got, ACROSS, 2, 2) + corner_b.astype(F32)], axis=0
        ).astype(LOW)
        return self.flip(across, 2), self.other_copy(other)

    def scatter_z(self, at, mine, got, across, other):
        own = self.part(at, mine, got, OWN) + across.astype(F32) + other.astype(F32)
        low = own.astype(LOW)
        return [own[0]] + [self.flip(low[k], 4 * k) for k in (1, 2, 3)]

    def scatter_end(self, at, parts):
        total = parts[0] + at[4].astype(F32)
        for value in parts[1:]:
            total = total + value.astype(F32)
        total = total.astype(LOW)
        away = self.other_copy(total)
        low = at[3] == 0
        return jnp.where(low, total, away).astype(F32), jnp.where(low, away, total).astype(F32)


def place():
    shard = lax.axis_index("fsdp")
    return jnp.stack(
        [shard // 4, (shard // 2) % 2, shard % 2, lax.axis_index("rep"), shard * 0]
    ).astype(jnp.int32)


AT = jax.ShapeDtypeStruct((5,), jnp.int32)
AT_SPEC = pl.BlockSpec(memory_space=pltpu.SMEM)


def hand_on(at, at_ref):
    for index in range(5):
        at_ref[index] = at[index]


def load_copies(plan, at, pieces, target, sem, rows, early):
    if len(pieces) == 1:
        return [pltpu.make_async_copy(pieces[0], target, sem)]
    half = rows // plan.shards // 2
    copies = []
    for piece, first, count, dz, dx, dc, dy in plan.piece_list(early):
        shard = (at[0] ^ dz) * 4 + (at[1] ^ dx) * 2 + (at[2] ^ dc)
        row = shard * 2 * half
        if dy is not None:
            row = row + (at[3] ^ dy) * half
        size = count * half
        copies.append(
            pltpu.make_async_copy(
                pieces[piece].at[pl.ds(first * half, size)], target.at[pl.ds(pl.multiple_of(row, half), size)], sem
            )
        )
    return copies


def fetch(plan, at, groups, sems):
    for index in range(len(groups)):
        for copy in load_copies(plan, at, *groups[index][:2], sems.at[index], *groups[index][2:]):
            copy.start()


def wait_for(plan, at, groups, sems, index):
    for copy in load_copies(plan, at, *groups[index][:2], sems.at[index], *groups[index][2:]):
        copy.wait()


def first_step(action):
    pl.when(pl.program_id(0) == 0)(action)


def project_kernel(plan, count, at, rows_ref, *refs):
    pieces, (out_ref, turned_ref, at_ref, weight, bias, sems) = refs[:count], refs[count:]
    depth = weight.shape[0]

    def load():
        hand_on(at, at_ref)
        groups = [(pieces, weight, weight.shape[0], True)]
        fetch(plan, at, groups, sems)
        wait_for(plan, at, groups, sems, 0)
        bias[...] = weight[:, 3 * depth :].astype(F32).T[:8]

    turned_ref[...] = rows_ref[...].T
    first_step(load)
    for block, row in ((0, 0), (1, None), (2, 1)):
        span = slice(block * depth, (block + 1) * depth)
        result = nn(rows_ref[...], weight[:, span])
        if row is not None:
            result = result + bias[row : row + 1]
        out_ref[:, span] = result.astype(LOW)


def project(plan, at, rows, pieces, depth, width, tile=256, after=()):
    count = len(pieces)
    height = rows.shape[0]
    return pl.pallas_call(
        later(functools.partial(project_kernel, plan, count), 1, after),
        out_shape=(jax.ShapeDtypeStruct((height, width), LOW), jax.ShapeDtypeStruct((depth, height), LOW), AT),
        grid_spec=pltpu.PrefetchScalarGridSpec(
            num_scalar_prefetch=1,
            grid=(height // tile,),
            in_specs=[ANY] * len(after)
            + [
                pl.BlockSpec((tile, depth), lambda i, at: (i, 0)),
            ]
            + [ANY] * count,
            out_specs=(
                pl.BlockSpec((tile, width), lambda i, at: (i, 0)),
                pl.BlockSpec((depth, tile), lambda i, at: (0, i)),
                AT_SPEC,
            ),
            scratch_shapes=[
                pltpu.VMEM((depth, width + EXTRA), LOW),
                pltpu.VMEM((8, depth), F32),
                pltpu.SemaphoreType.DMA((1,)),
            ],
        ),
        compiler_params=params(),
        cost_estimate=cost(2 * height * depth * width),
    )(at, *after, rows, *pieces)


def slot_rows(lengths_ref, block, row_count):
    along = lax.broadcasted_iota(jnp.int32, (1, row_count), 1)
    down = lax.broadcasted_iota(jnp.int32, (row_count, 1), 0)
    bound, lane_slot, row_slot = 0, jnp.zeros_like(along), jnp.zeros_like(down)
    for slot in range(SLOTS):
        bound = bound + lengths_ref[block, slot]
        lane_slot = lane_slot + (along >= bound).astype(jnp.int32)
        row_slot = row_slot + (down >= bound).astype(jnp.int32)
    return lane_slot, row_slot


def query_rows(lane_slot):
    line = lax.broadcasted_iota(jnp.int32, (8, lane_slot.shape[1]), 0)
    return jnp.where(line == lane_slot, -BIG, 0.0)


def key_columns(row_slot, offset):
    column = lax.broadcasted_iota(jnp.int32, (row_slot.shape[0], 128), 1) - offset
    barred = (column >= 0) & (column <= SLOTS) & ((column != row_slot) | (row_slot == SLOTS))
    return jnp.where(barred, 1.0, 0.0).astype(LOW)


def attend_kernel(lengths_ref, at, q_ref, k_ref, v_ref, out_ref, turned_ref, log_ref, at_ref):
    hand_on(at, at_ref)
    block = pl.program_id(0) // (H // 2 // PAIRS)
    row_count = q_ref.shape[0]
    lane_slot, row_slot = slot_rows(lengths_ref, block, row_count)
    inside = lane_slot < SLOTS
    lane = lax.broadcasted_iota(jnp.int32, (row_count, 128), 1)
    barred = query_rows(lane_slot).astype(LOW)
    padded = jnp.concatenate([barred, jnp.zeros((HD - 8, row_count), LOW)], axis=0)
    for pair in range(PAIRS):
        attend_pair(
            pair, inside, lane, row_slot, padded, q_ref, k_ref, v_ref, out_ref, turned_ref, log_ref
        )


def attend_pair(pair, inside, lane, row_slot, padded, q_ref, k_ref, v_ref, out_ref, turned_ref, log_ref):
    row_count = q_ref.shape[0]
    columns = slice(pair * 128, (pair + 1) * 128)
    q_turned = (q_ref[:, columns].astype(F32) * SCALE).T.astype(LOW)
    v_turned = v_ref[:, columns].astype(F32).T
    v_low = v_turned.astype(LOW)
    ones = jnp.ones((16, row_count), LOW)
    results = []
    for head in range(2):
        own = (lane < HD) if head == 0 else (lane >= HD)
        keyed = jnp.where(own, k_ref[:, columns], key_columns(row_slot, HD * (1 - head)))
        half = q_turned[head * HD : (head + 1) * HD]
        query = jnp.concatenate([half, padded] if head == 0 else [padded, half], axis=0)
        scores = nn(keyed, query)
        highest = jnp.max(scores, axis=0, keepdims=True)
        weights = jnp.exp(scores - highest)
        low = weights.astype(LOW)
        values = jnp.concatenate([v_low[head * HD : (head + 1) * HD], ones], axis=0)
        mixed = nn(values, low)
        total = mixed[HD : HD + 1]
        result = mixed[:HD] / total
        results.append(jnp.where(inside, result, v_turned[head * HD : (head + 1) * HD]))
        log_ref[0, 2 * pair + head : 2 * pair + head + 1] = jnp.where(inside, highest + jnp.log(total), BIG)
    turned = jnp.concatenate(results, axis=0)
    turned_ref[columns] = turned.astype(LOW)
    out_ref[:, columns] = turned.T.astype(LOW)


def attend(at, lengths, projected, after=()):
    rows = projected.shape[0]
    blocks, pairs = rows // CAP, H // 2 // PAIRS
    width = H * HD

    def column(part):
        return pl.BlockSpec((CAP, 128 * PAIRS), lambda i, n, at: (i // pairs, part * pairs + i % pairs))

    return pl.pallas_call(
        later(attend_kernel, 2, after),
        out_shape=(
            jax.ShapeDtypeStruct((rows, width), LOW),
            jax.ShapeDtypeStruct((width, rows), LOW),
            jax.ShapeDtypeStruct((blocks * pairs, 8, CAP), F32),
            AT,
        ),
        grid_spec=pltpu.PrefetchScalarGridSpec(
            num_scalar_prefetch=2,
            grid=(blocks * pairs,),
            in_specs=[ANY] * len(after) + [column(0), column(1), column(2)],
            out_specs=(
                column(0),
                pl.BlockSpec((128 * PAIRS, CAP), lambda i, n, at: (i % pairs, i // pairs)),
                pl.BlockSpec((1, 8, CAP), lambda i, n, at: (i, 0, 0)),
                AT_SPEC,
            ),
        ),
        compiler_params=params(),
        cost_estimate=cost(4 * rows * CAP * width, 12),
    )(lengths, at, *after, projected, projected, projected)


def three(value):
    first = value.astype(LOW).astype(F32)
    rest = value - first
    second = rest.astype(LOW).astype(F32)
    return first, second, rest - second


def attend_back_kernel(lengths_ref, at, q_ref, k_ref, v_ref, att_ref, grad_ref, log_ref, dq_ref, dk_ref, dv_ref, sums_ref, at_ref):
    hand_on(at, at_ref)
    block, step = pl.program_id(0) // (H // 2 // PAIRS), pl.program_id(0) % (H // 2 // PAIRS)
    row_count = q_ref.shape[0]
    lane_slot, row_slot = slot_rows(lengths_ref, block, row_count)
    outside = lane_slot >= SLOTS
    lane = lax.broadcasted_iota(jnp.int32, (row_count, 128), 1)
    barred = query_rows(lane_slot)
    refs = (q_ref, k_ref, v_ref, att_ref, grad_ref, log_ref, dq_ref, dk_ref, dv_ref, sums_ref)

    @first_step
    def _():
        sums_ref[...] = jnp.zeros_like(sums_ref)

    for pair in range(PAIRS):
        attend_back_pair(pair, step, row_slot, outside, lane, barred, *refs)


def attend_back_pair(
    pair, step, row_slot, outside, lane, barred, q_ref, k_ref, v_ref, att_ref, grad_ref, log_ref, dq_ref, dk_ref, dv_ref, sums_ref
):
    row_count = q_ref.shape[0]
    columns = slice(pair * 128, (pair + 1) * 128)
    q_scaled = (q_ref[:, columns].astype(F32) * SCALE)
    q_turned = q_scaled.T.astype(LOW)
    k_scaled = k_ref[:, columns].astype(F32) * SCALE
    k_turned = k_scaled.T.astype(LOW)
    grad_wide = grad_ref[:, columns].astype(F32).T
    grad_turned = grad_wide
    mixed = grad_turned * att_ref[columns].astype(F32)
    grad_turned = grad_turned.astype(LOW)
    line = lax.broadcasted_iota(jnp.int32, (8, row_count), 0)
    none = jnp.zeros((HD - 16, row_count), F32)

    def lines(value):
        first, second, third = three(value)
        return jnp.where(
            line == 0, -first, jnp.where(line == 1, -second, jnp.where(line == 2, -third, 0.0))
        )

    dqs, dks, dvs = [], [], []
    for head in range(2):
        own = (lane < HD) if head == 0 else (lane >= HD)
        start = HD * (1 - head)
        unit = (lane >= start + 8) & (lane < start + 11)
        keyed = jnp.where(own, k_ref[:, columns], jnp.where(unit, jnp.ones((), LOW), key_columns(row_slot, start)))
        valued = jnp.where(own, v_ref[:, columns], jnp.where(unit, jnp.ones((), LOW), jnp.zeros((), LOW)))
        extra = jnp.concatenate([barred, lines(log_ref[0, 2 * pair + head : 2 * pair + head + 1]), none], axis=0).astype(LOW)
        half = slice(head * HD, (head + 1) * HD)
        query = jnp.concatenate([q_turned[half], extra] if head == 0 else [extra, q_turned[half]], axis=0)
        weights = jnp.exp(nn(keyed, query))
        inner = jnp.sum(mixed[half], axis=0, keepdims=True)
        extra = jnp.concatenate([jnp.zeros_like(barred), lines(inner), none], axis=0).astype(LOW)
        grad = jnp.concatenate([grad_turned[half], extra] if head == 0 else [extra, grad_turned[half]], axis=0)
        moved = (weights * nn(valued, grad)).astype(LOW)
        dvs.append(nt(grad_turned[half], weights.astype(LOW)))
        dks.append(nt(q_turned[half], moved))
        dqs.append(nn(k_turned[half], moved))
    dq = jnp.concatenate(dqs, axis=0).T.astype(LOW)
    dq_ref[:, columns] = dq
    dk_ref[:, columns] = jnp.concatenate(dks, axis=0).T.astype(LOW)
    dv = jnp.concatenate(dvs, axis=0)
    dv = jnp.where(outside, dv + grad_wide, dv).T.astype(LOW)
    dv_ref[:, columns] = dv

    span = pl.ds(pl.multiple_of((step * PAIRS + pair) * 128, 128), 128)
    sums_ref[0:1, span] += jnp.sum(dq.astype(F32), axis=0, keepdims=True)
    sums_ref[1:2, span] += jnp.sum(dv.astype(F32), axis=0, keepdims=True)


def attend_back(at, lengths, projected, turned, grad_attended, logs, after=()):
    rows = projected.shape[0]
    blocks, pairs = rows // CAP, H // 2 // PAIRS
    width = H * HD

    def column(part):
        return pl.BlockSpec((CAP, 128 * PAIRS), lambda i, n, at: (i // pairs, part * pairs + i % pairs))

    return pl.pallas_call(
        later(attend_back_kernel, 2, after),
        out_shape=(jax.ShapeDtypeStruct((rows, width), LOW),) * 3 + (jax.ShapeDtypeStruct((8, width), F32), AT),
        grid_spec=pltpu.PrefetchScalarGridSpec(
            num_scalar_prefetch=2,
            grid=(blocks * pairs,),
            in_specs=[ANY] * len(after)
            + [
                column(0), column(1), column(2),
                pl.BlockSpec((128 * PAIRS, CAP), lambda i, n, at: (i % pairs, i // pairs)),
                column(0),
                pl.BlockSpec((1, 8, CAP), lambda i, n, at: (i, 0, 0)),
            ],
            out_specs=(column(0),) * 3 + (pl.BlockSpec((8, width), lambda i, n, at: (0, 0)), AT_SPEC),
        ),
        compiler_params=params(),
        cost_estimate=cost(10 * rows * CAP * width, 5),
    )(lengths, at, *after, projected, projected, projected, turned, grad_attended, logs)


def norm(values):
    centre = jnp.mean(values, axis=-1, keepdims=True)
    centred = values - centre
    scale = lax.rsqrt(jnp.mean(centred * centred, axis=-1, keepdims=True) + EPSILON)
    return centred * scale, scale


def norm_back(grad, normal, scale):
    return scale * (
        grad
        - jnp.mean(grad, axis=-1, keepdims=True)
        - normal * jnp.mean(grad * normal, axis=-1, keepdims=True)
    )


ROOT_HALF = 0.7071067811865476
ROOT_TAU = 0.3989422804014327


def up_kernel(plan, chunk, at, rows_ref, att_ref, *refs):
    pieces = refs[:-11]
    (
        active_ref, slope_ref, normal_ref, scale_ref, first_ref, turned_ref, small_ref, at_ref, w_wide, wide_ref, sems,
    ) = refs[-11:]
    depth = w_wide.shape[0]
    hidden = w_wide.shape[1] - depth - EXTRA
    groups = [(pieces, w_wide, depth, False)]

    def load():
        hand_on(at, at_ref)
        fetch(plan, at, groups, sems)
        wait_for(plan, at, groups, sems, 0)
        table = w_wide[:, hidden + depth :].astype(F32).T
        small_ref[...] = table[:8]
        part = depth // plan.shards
        for shard in range(plan.shards):
            for line in range(hidden // depth):
                start = (shard * (hidden // depth) + line) * part
                wide_ref[0:1, start : start + part] = table[8 + line : 9 + line, shard * part : (shard + 1) * part]

    first_step(load)

    def small(index):
        return small_ref[index : index + 1]

    residual = rows_ref[...].astype(F32) + nn(att_ref[...], w_wide[:, hidden : hidden + depth]) + small(0)
    normal, scale = norm(residual)
    normal_ref[...] = normal.astype(LOW)
    scale_ref[...] = jnp.broadcast_to(scale, scale_ref.shape)
    first = normal * small(2) + small(3)
    first_ref[...] = first
    low = first.astype(LOW)
    turned_ref[...] = low.T
    for start in range(0, hidden, chunk):
        span = slice(start, start + chunk)
        wide = nn(low, w_wide[:, span]) + wide_ref[0:1, span]
        cumulative = 0.5 * (1.0 + lax.erf(wide * ROOT_HALF))
        active_ref[:, span] = (wide * cumulative).astype(LOW)
        slope_ref[:, span] = (cumulative + wide * (ROOT_TAU * jnp.exp(-0.5 * wide * wide))).astype(LOW)


def tiled(tile, width):
    return pl.BlockSpec((tile, width), lambda i, at: (i, 0))


def turned_tile(tile, width):
    return pl.BlockSpec((width, tile), lambda i, at: (0, i))


def whole_block(height, width):
    return pl.BlockSpec((height, width), lambda i, at: (0, 0))


def up(plan, at, rows, attended, hidden, pieces, tile=256, chunk=1024, after=()):
    height, depth = rows.shape
    return pl.pallas_call(
        later(functools.partial(up_kernel, plan, chunk), 1, after),
        out_shape=(
            jax.ShapeDtypeStruct((height, hidden), LOW),
            jax.ShapeDtypeStruct((height, hidden), LOW),
            jax.ShapeDtypeStruct((height, depth), LOW),
            jax.ShapeDtypeStruct((height, 128), F32),
            jax.ShapeDtypeStruct((height, depth), F32),
            jax.ShapeDtypeStruct((depth, height), LOW),
            jax.ShapeDtypeStruct((8, depth), F32),
            AT,
        ),
        grid_spec=pltpu.PrefetchScalarGridSpec(
            num_scalar_prefetch=1,
            grid=(height // tile,),
            in_specs=[ANY] * len(after) + [tiled(tile, depth), tiled(tile, depth)] + [ANY] * len(pieces),
            out_specs=(
                tiled(tile, hidden), tiled(tile, hidden), tiled(tile, depth), tiled(tile, 128),
                tiled(tile, depth), turned_tile(tile, depth), whole_block(8, depth), AT_SPEC,
            ),
            scratch_shapes=[
                pltpu.VMEM((depth, hidden + depth + EXTRA), LOW),
                pltpu.VMEM((8, hidden), F32),
                pltpu.SemaphoreType.DMA((1,)),
            ],
        ),
        compiler_params=params(),
        cost_estimate=cost(2 * height * depth * (depth + hidden)),
    )(at, *after, rows, attended, *pieces)


def over_kernel(plan, chunk, at, first_ref, active_ref, cot_ref, small_ref, *refs):
    pieces = refs[:-6]
    result_ref, second_ref, sums_ref, at_ref, w_contract, sems = refs[-6:]
    hidden = w_contract.shape[0]
    groups = [(pieces, w_contract, hidden, False)]

    def load():
        hand_on(at, at_ref)
        fetch(plan, at, groups, sems)
        sums_ref[...] = jnp.zeros_like(sums_ref)
        wait_for(plan, at, groups, sems, 0)

    first_step(load)

    def small(index):
        return small_ref[index : index + 1].astype(F32)

    def add(index, value):
        sums_ref[index : index + 1] += jnp.sum(value, axis=0, keepdims=True)

    normal, scale = norm(first_ref[...] + small(1) + nn(active_ref[...], w_contract[...]))
    result_ref[...] = (normal * small(4) + small(5)).astype(LOW)
    cot = cot_ref[...].astype(F32)
    add(4, cot * normal)
    add(5, cot)
    second = norm_back(cot * small(4), normal, scale).astype(LOW)
    second_ref[...] = second
    add(1, second.astype(F32))


def over(plan, at, first, active, cot, small, pieces, tile=256, chunk=1024, after=()):
    height, depth = first.shape
    hidden = active.shape[1]
    return pl.pallas_call(
        later(functools.partial(over_kernel, plan, chunk), 1, after),
        out_shape=(
            jax.ShapeDtypeStruct((height, depth), LOW),
            jax.ShapeDtypeStruct((height, depth), LOW),
            jax.ShapeDtypeStruct((8, depth), F32),
            AT,
        ),
        grid_spec=pltpu.PrefetchScalarGridSpec(
            num_scalar_prefetch=1,
            grid=(height // tile,),
            in_specs=[ANY] * len(after)
            + [tiled(tile, depth), tiled(tile, hidden), tiled(tile, depth), whole_block(8, depth)]
            + [ANY] * len(pieces),
            out_specs=(
                tiled(tile, depth), tiled(tile, depth), whole_block(8, depth), AT_SPEC,
            ),
            scratch_shapes=[pltpu.VMEM((hidden, depth), LOW), pltpu.SemaphoreType.DMA((1,))],
        ),
        compiler_params=params(),
        cost_estimate=cost(2 * height * depth * hidden),
    )(at, *after, first, active, cot, small, *pieces)


def down_kernel(plan, counts, chunk, at, second_ref, slope_ref, normal_ref, scale_ref, small_ref, *refs):
    first_count, second_count = counts
    wide_pieces, contract_pieces = refs[:first_count], refs[first_count : first_count + second_count]
    expanded_ref, branch_ref, grad_att_ref, sums_ref, wide_sums_ref, at_ref, w_wide, w_contract, sems = refs[
        first_count + second_count :
    ]
    hidden, depth = w_contract.shape

    groups = [(contract_pieces, w_contract, hidden, False), (wide_pieces, w_wide, depth, False)]

    def load():
        hand_on(at, at_ref)
        fetch(plan, at, groups, sems)
        sums_ref[...] = jnp.zeros_like(sums_ref)
        wide_sums_ref[...] = jnp.zeros_like(wide_sums_ref)
        wait_for(plan, at, groups, sems, 0)

    first_step(load)

    def add(index, value):
        sums_ref[index : index + 1] += jnp.sum(value, axis=0, keepdims=True)

    second = second_ref[...]
    total = second.astype(F32)
    for start in range(0, hidden, chunk):
        span = slice(start, start + chunk)
        grad = (nt(second, w_contract[span]) * slope_ref[:, span].astype(F32)).astype(LOW)
        expanded_ref[:, span] = grad
        wide_sums_ref[0:1, span] += jnp.sum(grad.astype(F32), axis=0, keepdims=True)
        if start == 0:
            first_step(lambda: wait_for(plan, at, groups, sems, 1))
        total = total + nt(grad, w_wide[:, span])
    normal = normal_ref[...].astype(F32)
    add(2, total * normal)
    add(3, total)
    branch = norm_back(total * small_ref[2:3].astype(F32), normal, scale_ref[:, 0:1]).astype(LOW)
    branch_ref[...] = branch
    add(0, branch.astype(F32))
    grad_att_ref[...] = nt(branch, w_wide[:, hidden : hidden + depth]).astype(LOW)


def down(plan, at, second, slope, normal, scale, small, wide_pieces, contract_pieces, tile=256, chunk=1024, after=()):
    height, depth = second.shape
    hidden = slope.shape[1]

    def tiled(width):
        return pl.BlockSpec((tile, width), lambda i, at: (i, 0))

    def whole(height, width):
        return pl.BlockSpec((height, width), lambda i, at: (0, 0))

    return pl.pallas_call(
        later(functools.partial(down_kernel, plan, (len(wide_pieces), len(contract_pieces)), chunk), 1, after),
        out_shape=(
            jax.ShapeDtypeStruct((height, hidden), LOW),
            jax.ShapeDtypeStruct((height, depth), LOW),
            jax.ShapeDtypeStruct((height, depth), LOW),
            jax.ShapeDtypeStruct((8, depth), F32),
            jax.ShapeDtypeStruct((8, hidden), F32),
            AT,
        ),
        grid_spec=pltpu.PrefetchScalarGridSpec(
            num_scalar_prefetch=1,
            grid=(height // tile,),
            in_specs=[ANY] * len(after)
            + [tiled(depth), tiled(hidden), tiled(depth), tiled(128), whole(8, depth)]
            + [ANY] * (len(wide_pieces) + len(contract_pieces)),
            out_specs=(tiled(hidden), tiled(depth), tiled(depth), whole(8, depth), whole(8, hidden), AT_SPEC),
            scratch_shapes=[
                pltpu.VMEM((depth, hidden + depth + EXTRA), LOW),
                pltpu.VMEM((hidden, depth), LOW),
                pltpu.SemaphoreType.DMA((2,)),
            ],
        ),
        compiler_params=params(),
        cost_estimate=cost(2 * height * depth * (depth + 2 * hidden)),
    )(at, *after, second, slope, normal, scale, small, *wide_pieces, *contract_pieces)


def source(at, flip, group, k):
    shard = (at[0] ^ k) * 4 + (at[1] ^ (group % 2)) * 2 + (at[2] ^ flip)
    return shard * 2 + (at[3] ^ (group // 2))


def outer_tall_kernel(at, left, right, out, at_ref):
    hand_on(at, at_ref)
    out[...] = tn(left[...], right[...]).astype(LOW)


def outer_tall(at, left, right, tile=512, after=()):
    height, rows = left.shape
    width = right.shape[1]
    return pl.pallas_call(
        later(outer_tall_kernel, 1, after),
        out_shape=(jax.ShapeDtypeStruct((rows, width), LOW), AT),
        grid_spec=pltpu.PrefetchScalarGridSpec(
            num_scalar_prefetch=1,
            grid=(rows // tile,),
            in_specs=[ANY] * len(after)
            + [pl.BlockSpec((height, tile), lambda i, at: (0, i)), whole_block(height, width)],
            out_specs=(tiled(tile, width), AT_SPEC),
        ),
        compiler_params=params(),
        cost_estimate=cost(2 * height * rows * width),
    )(at, *after, left, right)


def outer_row_kernel(count, tile, at, turned, extra, *refs):
    rights, (out, at_ref) = refs[:count], refs[count:]
    step = pl.program_id(0)
    total = out.shape[1] - EXTRA
    steps = total // tile // count
    for place in range(count * steps):

        @pl.when(step == place)
        def _(place=place):
            out[:, place * tile : (place + 1) * tile] = nn(turned[...], rights[place // steps][...]).astype(LOW)

    @first_step
    def _():
        hand_on(at, at_ref)
        lines = jnp.zeros((EXTRA - extra.shape[0], extra.shape[1]), F32)
        out[:, total:] = jnp.concatenate([extra[...], lines], axis=0).T.astype(LOW)


def outer_row(at, turned, rights, extra, tile=512, after=()):
    rows, height = turned.shape
    steps = rights[0].shape[1] // tile
    count = len(rights)
    width = count * steps * tile

    def column(index):
        return pl.BlockSpec((height, tile), lambda i, at: (0, jnp.clip(i - index * steps, 0, steps - 1)))

    return pl.pallas_call(
        later(functools.partial(outer_row_kernel, count, tile), 1, after),
        out_shape=(jax.ShapeDtypeStruct((rows, width + EXTRA), LOW), AT),
        grid_spec=pltpu.PrefetchScalarGridSpec(
            num_scalar_prefetch=1,
            grid=(count * steps,),
            in_specs=[ANY] * len(after)
            + [whole_block(rows, height), whole_block(*extra.shape)]
            + [column(index) for index in range(count)],
            out_specs=(whole_block(rows, width + EXTRA), AT_SPEC),
        ),
        compiler_params=params(),
        cost_estimate=cost(2 * height * rows * width),
    )(at, *after, turned, extra, *rights)


def outer_wide_kernel(flip, owners, firsts, tile, extra, at, *refs):
    count = max(owners) + 1
    turned, rights = refs[:count], refs[count : count + len(owners)]
    if extra:
        extra_ref, out, at_ref, lines, held, sem = refs[-6:]
    else:
        out, at_ref, held, sem = refs[-4:]
    step = pl.program_id(0)
    half = held.shape[1] // 16

    def load():
        hand_on(at, at_ref)
        copies = []
        for index, ref in enumerate(turned):
            for group in range(4):
                for k in range(4):
                    row = pl.multiple_of(source(at, flip, group, k) * half, half)
                    copies.append(
                        pltpu.make_async_copy(
                            ref.at[pl.ds(row, half)], held.at[index, pl.ds((group * 4 + k) * half, half)], sem
                        )
                    )
        for copy in copies:
            copy.start()
        for copy in copies:
            copy.wait()

    first_step(load)
    if extra:
        @first_step
        def _():
            rest = jnp.zeros((EXTRA - extra_ref.shape[0], extra_ref.shape[1]), F32)
            lines[...] = jnp.concatenate([extra_ref[...], rest], axis=0).T.astype(LOW)
            for group in range(4):
                for k in range(4):
                    row = pl.multiple_of(source(at, flip, group, k) * half, half)
                    out[group * 4 + k, :, tile * firsts[-1] :] = lines[pl.ds(row, half), :]

    for index, owner in enumerate(owners):
        if extra:
            for place in range(firsts[index], firsts[index + 1]):

                @pl.when(step == place)
                def _(index=index, owner=owner, place=place):
                    result = nn(held[owner], rights[index][...]).astype(LOW)
                    out[:, :, place * tile : (place + 1) * tile] = result.reshape(16, half, tile)

            continue

        @pl.when((step >= firsts[index]) & (step < firsts[index + 1]))
        def _(index=index, owner=owner):
            result = nn(held[owner], rights[index][...]).astype(LOW)
            out[...] = result.reshape(out.shape)


def outer_wide(at, turned, rights, owners, flip, tile=1024, extra=None, after=()):
    rows, height = turned[0].shape
    half = rows // 32
    counts = [right.shape[1] // tile for right in rights]
    firsts = [sum(counts[:i]) for i in range(len(counts) + 1)]
    width = tile * firsts[-1]
    more = [] if extra is None else [extra]
    wide = width + EXTRA * len(more)
    block = pl.BlockSpec((16, half, tile), lambda i, at: (0, 0, i))
    if more:
        block = pl.BlockSpec((16, half, wide), lambda i, at: (0, 0, 0))

    def column(index):
        return pl.BlockSpec((height, tile), lambda i, at: (0, jnp.clip(i - firsts[index], 0, counts[index] - 1)))

    return pl.pallas_call(
        later(functools.partial(outer_wide_kernel, flip, tuple(owners), tuple(firsts), tile, bool(more)), 1, after),
        out_shape=(jax.ShapeDtypeStruct((16, half, wide), LOW), AT),
        grid_spec=pltpu.PrefetchScalarGridSpec(
            num_scalar_prefetch=1,
            grid=(firsts[-1],),
            in_specs=[ANY] * len(after)
            + [ANY] * len(turned)
            + [column(index) for index in range(len(rights))]
            + [whole_block(*line.shape) for line in more],
            out_specs=(block, AT_SPEC),
            scratch_shapes=[pltpu.VMEM((rows, EXTRA), LOW) for line in more]
            + [pltpu.VMEM((len(turned), rows // 2, height), LOW), pltpu.SemaphoreType.DMA],
        ),
        compiler_params=params(),
        cost_estimate=cost(height * rows * width),
    )(at, *after, *turned, *rights, *more)


def owned_sum(whole):
    return lax.psum_scatter(whole, "fsdp", scatter_dimension=0, tiled=True)


def copies_sum(plan, at, owned):
    if plan.copies == 2:
        owned = owned + at[4].astype(LOW)
        return owned.astype(F32) + plan.other_copy(owned).astype(F32)
    return lax.psum(owned, "rep").astype(F32)


def back_kernel(plan, count, at, branch_ref, dq_ref, dk_ref, dv_ref, *refs):
    pieces, (out_ref, at_ref, weight, sems) = refs[:count], refs[count:]
    width = dq_ref.shape[1]

    def load():
        hand_on(at, at_ref)
        groups = [(pieces, weight, weight.shape[0], True)]
        fetch(plan, at, groups, sems)
        wait_for(plan, at, groups, sems, 0)

    first_step(load)

    total = branch_ref[...].astype(F32)
    for index, ref in enumerate((dq_ref, dk_ref, dv_ref)):
        total = total + nt(ref[...], weight[:, index * width : (index + 1) * width])
    out_ref[...] = total.astype(LOW)


def back(plan, at, branch, dq, dk, dv, pieces, tile=256, after=()):
    count = len(pieces)
    height, depth = branch.shape
    width = dq.shape[1]
    tiled = pl.BlockSpec((tile, depth), lambda i, at: (i, 0))
    return pl.pallas_call(
        later(functools.partial(back_kernel, plan, count), 1, after),
        out_shape=(jax.ShapeDtypeStruct((height, depth), LOW), AT),
        grid_spec=pltpu.PrefetchScalarGridSpec(
            num_scalar_prefetch=1,
            grid=(height // tile,),
            in_specs=[ANY] * len(after)
            + [tiled] * 4 + [ANY] * count,
            out_specs=(tiled, AT_SPEC),
            scratch_shapes=[pltpu.VMEM((depth, 3 * width + EXTRA), LOW), pltpu.SemaphoreType.DMA((1,))],
        ),
        compiler_params=params(),
        cost_estimate=cost(6 * height * depth * width),
    )(at, *after, branch, dq, dk, dv, *pieces)


def body(
    tokens, seq_lengths, out_cotangent, project_in, project_out, expand, contract,
    query_bias, value_bias, out_bias, expand_bias, contract_bias,
    first_gain, first_shift, second_gain, second_shift,
    *, shards, copies,
):
    plan = Plan(shards, copies)
    at = place()
    depth = tokens.shape[1]
    hidden = expand.shape[1]
    part, wide_part = query_bias.shape[0], expand_bias.shape[0]

    def columns(*vectors):
        table = jnp.stack([vector for vector in vectors], axis=1)
        return jnp.pad(table, ((0, 0), (0, EXTRA - len(vectors))))

    zero = jnp.zeros_like(query_bias)
    in_shard = jnp.concatenate([project_in, columns(query_bias, value_bias)], axis=1)
    wide_bias = tuple(expand_bias[i * part : (i + 1) * part] for i in range(wide_part // part))
    small = (out_bias, contract_bias, first_gain, first_shift, second_gain, second_shift, zero, zero)
    wide_shard = jnp.concatenate([expand, project_out, columns(*small, *wide_bias)], axis=1)
    width = project_in.shape[1]
    if plan.split:
        in_beside, in_parts = plan.gather_z(at, in_shard, True)
        in_far, in_across, in_other = plan.gather_xy(at, in_shard, in_parts, True)
        unused, wide_parts = plan.gather_z(pinned(at, in_parts[2]), wide_shard)
        in_corners = plan.gather_corner(at, in_shard, in_across, in_other, True)
        in_main = (in_shard, in_beside, in_far, in_across, in_other)
        at_wide = pinned(at, *wide_parts)
        in_cores = plan.gather_core(at, *in_main) + plan.gather_core(at_wide, *in_corners)
        in_pieces = list(in_main + in_corners) + in_cores
        at_core = at_wide
        wide_far, wide_across, wide_other = plan.gather_xy(at_core, wide_shard, wide_parts)
        contract_pieces = [lax.all_gather(contract + pinned(at_core, wide_across, wide_other)[4].astype(LOW), "fsdp", axis=0, tiled=True)]
        wide_corners = plan.gather_corner(at_core, wide_shard, wide_across, wide_other)
    else:
        in_pieces, wide_pieces, contract_pieces = (
            [lax.all_gather(shard, "fsdp", axis=0, tiled=True)] for shard in (in_shard, wide_shard, contract)
        )
    first_after = [wide_across, wide_other] if plan.split else []
    projected, tokens_turned, at = project(plan, at, tokens, in_pieces, depth, width, after=first_after)
    if plan.split:
        wide_main = (wide_shard, wide_far, wide_across, wide_other)
        attended, attended_turned, logs, at = attend(at, seq_lengths, projected, after=wide_corners)
        wide_pieces = list(wide_main + wide_corners)
        wide_pieces += plan.gather_core(at, *wide_main) + plan.gather_core(at, *wide_corners)
    else:
        attended, attended_turned, logs, at = attend(at, seq_lengths, projected)
    active, slope, normal, scale, first, first_turned, table, at = up(plan, at, tokens, attended, hidden, wide_pieces)
    result, second, sums, at = over(plan, at, first, active, out_cotangent, table, contract_pieces)
    whole, at = outer_tall(at, active, second)
    contract_owned = owned_sum(whole)
    grad_expanded, branch, grad_attended, more_sums, wide_sums, at = down(
        plan, at, second, slope, normal, scale, table, wide_pieces, contract_pieces
    )
    lines = wide_sums[0].reshape(shards, wide_part // part, part).transpose(1, 0, 2).reshape(-1, depth)
    lines = jnp.concatenate([sums[:6] + more_sums[:6], lines], axis=0)
    lines = jnp.pad(lines, ((0, 14 - lines.shape[0]), (0, 0)))
    if plan.split:
        turned, rights, owners = (first_turned, attended_turned), (grad_expanded, branch), (0, 1)
        theirs, at = outer_wide(at, turned, rights, owners, 1)
        e_got = plan.flip(theirs, 1)
        e_mine, at = outer_wide(at, turned, rights, owners, 0)
        e_corners = plan.scatter_corner(at, e_mine, e_got)
        dq, dk, dv, back_sums, at = attend_back(at, seq_lengths, projected, attended_turned, grad_attended, logs)
        e_across, e_other = plan.scatter_xy(at, e_mine, e_got, *e_corners)
        extra = jnp.concatenate([back_sums[:2], lines], axis=0)
        turned, rights, owners = (tokens_turned,), (dq, dk, dv), (0, 0, 0)
        theirs, at = outer_wide(at, turned, rights, owners, 1, extra=extra, after=[*e_corners, contract_owned])
        contract_sum = copies_sum(plan, at, contract_owned)
        i_got = plan.flip(theirs, 1)
        i_mine, at = outer_wide(at, turned, rights, owners, 0, extra=extra)
        e_parts = plan.scatter_z(at, e_mine, e_got, e_across, e_other)
        i_corners = plan.scatter_corner(at, i_mine, i_got)
        grad_tokens, at = back(plan, at, branch, dq, dk, dv, in_pieces, after=[i_got])
        i_across, i_other = plan.scatter_xy(at, i_mine, i_got, *i_corners)
        e_ends = plan.scatter_end(at, e_parts)
        i_parts = plan.scatter_z(at, i_mine, i_got, i_across, i_other)
        owned = jnp.concatenate(plan.scatter_end(at, i_parts), axis=0)
        grad_wide = jnp.concatenate(e_ends, axis=0)
        grad_expand, grad_project_out = grad_wide[:, :hidden], grad_wide[:, hidden:]
    else:
        none = jnp.zeros((8, depth), F32)
        whole, at = outer_row(at, first_turned, (grad_expanded,), none)
        grad_expand = copies_sum(plan, at, owned_sum(whole))[:, :hidden]
        whole, at = outer_row(at, attended_turned, (branch,), none)
        grad_project_out = copies_sum(plan, at, owned_sum(whole))[:, :depth]
        dq, dk, dv, back_sums, at = attend_back(at, seq_lengths, projected, attended_turned, grad_attended, logs)
        extra = jnp.concatenate([back_sums[:2], lines], axis=0)
        whole, at = outer_row(at, tokens_turned, (dq, dk, dv), extra)
        owned = copies_sum(plan, at, owned_sum(whole))
        contract_sum = copies_sum(plan, at, contract_owned)
        grad_tokens, at = back(plan, at, branch, dq, dk, dv, in_pieces)
    grad_contract = contract_sum
    grad_project_in = owned[:, :width]
    small = owned[:, width : width + 8 + wide_part // part].T
    grad_query, grad_value, grad_out, grad_down, gain_one, shift_one, gain_two, shift_two = (small[i] for i in range(8))
    grad_wide_bias = small[8:].reshape(-1)
    return (
        result, grad_tokens, grad_project_in, grad_project_out, grad_expand, grad_contract,
        grad_query, grad_value, grad_out, grad_wide_bias, grad_down,
        gain_one, shift_one, gain_two, shift_two,
    )


def solution(mesh):
    split, row, vector = P(("fsdp", "rep"), None), P("fsdp", None), P("fsdp")
    return jax.shard_map(
        functools.partial(body, shards=mesh.shape["fsdp"], copies=mesh.shape["rep"]),
        mesh=mesh,
        in_specs=(split,) * 3 + (row,) * 4 + (vector,) * 9,
        out_specs=(split,) * 2 + (row,) * 4 + (vector,) * 9,
        check_vma=False,
    )
```

```python
import functools

import jax
import jax.numpy as jnp
from jax import lax
from jax.experimental import pallas as pl
from jax.experimental.pallas import tpu as pltpu
from jax.sharding import PartitionSpec as P

H = 16
HD = 64
SLOTS = 4
CAP = 512
EPSILON = 1e-12
SCALE = 0.125
BIG = 1e30
PAIRS = 4
EXTRA = 128
HASTE = 1
LOW = jnp.bfloat16
F32 = jnp.float32
VMEM_LIMIT = 60 * 1024 * 1024
ANY = pl.BlockSpec(memory_space=pl.ANY)
OWN, ACROSS, OTHER, CORNER = (0, 0), (1, 0), (0, 1), (1, 1)
GROUPS = (OWN, ACROSS, OTHER, CORNER)


def params(limit=VMEM_LIMIT):
    return pltpu.CompilerParams(vmem_limit_bytes=limit, dimension_semantics=("arbitrary",))


def cost(flops, slow=2):
    return pl.CostEstimate(flops=slow * flops // HASTE, bytes_accessed=slow * flops // HASTE // 320, transcendentals=0)


def later(kernel, prefetch, after):
    def run(*refs):
        kernel(*refs[:prefetch], *refs[prefetch + len(after) :])

    return run


def dot(left, right, over):
    return lax.dot_general(left, right, ((over[:1], over[1:]), ((), ())), preferred_element_type=F32)


def nn(left, right):
    return dot(left, right, (1, 0))


def nt(left, right):
    return dot(left, right, (1, 1))


def tn(left, right):
    return dot(left, right, (0, 0))


def pinned(at, *values):
    for value in values:
        sample = jnp.clip(value[(0,) * value.ndim].astype(F32), -1.0, 1.0).astype(jnp.int32)
        at = at + jnp.minimum(jnp.abs(sample), 0)
    return at


class Plan:
    def __init__(self, shards, copies):
        self.shards, self.copies = shards, copies
        self.split = shards == 16 and copies == 2

    def flip(self, value, bits):
        return lax.ppermute(value, "fsdp", [(i, i ^ bits) for i in range(self.shards)])

    def other_copy(self, value):
        return lax.ppermute(value, "rep", [(0, 1), (1, 0)])


    def gather_z(self, at, shard, early=False):
        half = shard.shape[0] // 2
        own = lax.dynamic_slice_in_dim(shard, at[3] * half, half, 0)
        beside = self.flip(shard, 2) if early else None
        return beside, [self.flip(own, 4 * k) for k in (1, 2, 3)]

    def gather_xy(self, at, shard, far, early=False):
        half = shard.shape[0] // 2
        far = jnp.concatenate([part + at[4].astype(LOW) for part in far], axis=0)
        own = lax.dynamic_slice_in_dim(shard, at[3] * half, half, 0)
        across = far if early else jnp.concatenate([own, far], axis=0)
        return far, self.flip(across, 2), self.other_copy(far)

    def gather_corner(self, at, shard, across, other, early=False):
        half = shard.shape[0] // 2
        left = lax.dynamic_slice_in_dim(other, at[4], half, 0)
        if not early:
            left = jnp.concatenate([lax.dynamic_slice_in_dim(shard, (1 - at[3]) * half, half, 0), left], axis=0)
        start = across.shape[0] - 2 * half
        return self.flip(left, 2), self.other_copy(lax.dynamic_slice_in_dim(across, start + at[4], 2 * half, 0))

    def gather_core(self, at, *pieces):
        return [self.flip(jnp.concatenate([piece + at[4].astype(LOW) for piece in pieces], axis=0), 1)]

    def piece_list(self, early):
        blocks = [[(0, 0, None)]]
        if early:
            blocks.append([(0, 1, None)])
        blocks.append([(k, 0, 0) for k in (1, 2, 3)])
        blocks.append([(k, 1, 0) for k in ((1, 2, 3) if early else (0, 1, 2, 3))])
        blocks.append([(k, 0, 1) for k in (1, 2, 3)])
        blocks.append([(k, 1, 1) for k in ((1,) if early else (0, 1))])
        blocks.append([(k, 1, 1) for k in (2, 3)])
        main = len(blocks) - 2
        out, first = [], 0
        for core in (0, 1):
            for piece, content in enumerate(blocks):
                if core == 0 or piece in (0, main):
                    first = 0
                for dz, dx, dy in content:
                    size = 2 if dy is None else 1
                    at_piece = piece if core == 0 else len(blocks) + (piece >= main)
                    out.append((at_piece, first, size, dz, dx, core, dy))
                    first += size
        return out


    def part(self, at, mine, got, group, first=0, count=4):
        start = GROUPS.index(group) * 4 + first
        stop = start + count
        return mine[start:stop].astype(F32) + got[start:stop].astype(F32) + at[4].astype(F32)

    def scatter_corner(self, at, mine, got):
        return (
            self.flip(self.part(at, mine, got, CORNER, 0, 2).astype(LOW), 2),
            self.other_copy(self.part(at, mine, got, CORNER, 2, 2).astype(LOW)),
        )

    def scatter_xy(self, at, mine, got, corner_a, corner_b):
        other = jnp.concatenate(
            [self.part(at, mine, got, OTHER, 0, 2) + corner_a.astype(F32), self.part(at, mine, got, OTHER, 2, 2)], axis=0
        ).astype(LOW)
        across = jnp.concatenate(
            [self.part(at, mine, got, ACROSS, 0, 2), self.part(at, mine, got, ACROSS, 2, 2) + corner_b.astype(F32)], axis=0
        ).astype(LOW)
        return self.flip(across, 2), self.other_copy(other)

    def scatter_z(self, at, mine, got, across, other):
        own = self.part(at, mine, got, OWN) + across.astype(F32) + other.astype(F32)
        low = own.astype(LOW)
        return [own[0]] + [self.flip(low[k], 4 * k) for k in (1, 2, 3)]

    def scatter_end(self, at, parts):
        total = parts[0] + at[4].astype(F32)
        for value in parts[1:]:
            total = total + value.astype(F32)
        total = total.astype(LOW)
        away = self.other_copy(total)
        low = at[3] == 0
        return jnp.where(low, total, away).astype(F32), jnp.where(low, away, total).astype(F32)


def place():
    shard = lax.axis_index("fsdp")
    return jnp.stack(
        [shard // 4, (shard // 2) % 2, shard % 2, lax.axis_index("rep"), shard * 0]
    ).astype(jnp.int32)


AT = jax.ShapeDtypeStruct((5,), jnp.int32)
AT_SPEC = pl.BlockSpec(memory_space=pltpu.SMEM)


def hand_on(at, at_ref):
    for index in range(5):
        at_ref[index] = at[index]


def load_copies(plan, at, pieces, target, sem, rows, early):
    if len(pieces) == 1:
        return [pltpu.make_async_copy(pieces[0], target, sem)]
    half = rows // plan.shards // 2
    copies = []
    for piece, first, count, dz, dx, dc, dy in plan.piece_list(early):
        shard = (at[0] ^ dz) * 4 + (at[1] ^ dx) * 2 + (at[2] ^ dc)
        row = shard * 2 * half
        if dy is not None:
            row = row + (at[3] ^ dy) * half
        size = count * half
        copies.append(
            pltpu.make_async_copy(
                pieces[piece].at[pl.ds(first * half, size)], target.at[pl.ds(pl.multiple_of(row, half), size)], sem
            )
        )
    return copies


def fetch(plan, at, groups, sems):
    for index in range(len(groups)):
        for copy in load_copies(plan, at, *groups[index][:2], sems.at[index], *groups[index][2:]):
            copy.start()


def wait_for(plan, at, groups, sems, index):
    for copy in load_copies(plan, at, *groups[index][:2], sems.at[index], *groups[index][2:]):
        copy.wait()


def first_step(action):
    pl.when(pl.program_id(0) == 0)(action)


def project_kernel(plan, count, at, rows_ref, *refs):
    pieces, (out_ref, turned_ref, at_ref, weight, bias, sems) = refs[:count], refs[count:]
    depth = weight.shape[0]

    def load():
        hand_on(at, at_ref)
        groups = [(pieces, weight, weight.shape[0], True)]
        fetch(plan, at, groups, sems)
        wait_for(plan, at, groups, sems, 0)
        bias[...] = weight[:, 3 * depth :].astype(F32).T[:8]

    turned_ref[...] = rows_ref[...].T
    first_step(load)
    for block, row in ((0, 0), (1, None), (2, 1)):
        span = slice(block * depth, (block + 1) * depth)
        result = nn(rows_ref[...], weight[:, span])
        if row is not None:
            result = result + bias[row : row + 1]
        out_ref[:, span] = result.astype(LOW)


def project(plan, at, rows, pieces, depth, width, tile=256, after=()):
    count = len(pieces)
    height = rows.shape[0]
    return pl.pallas_call(
        later(functools.partial(project_kernel, plan, count), 1, after),
        out_shape=(jax.ShapeDtypeStruct((height, width), LOW), jax.ShapeDtypeStruct((depth, height), LOW), AT),
        grid_spec=pltpu.PrefetchScalarGridSpec(
            num_scalar_prefetch=1,
            grid=(height // tile,),
            in_specs=[ANY] * len(after)
            + [
                pl.BlockSpec((tile, depth), lambda i, at: (i, 0)),
            ]
            + [ANY] * count,
            out_specs=(
                pl.BlockSpec((tile, width), lambda i, at: (i, 0)),
                pl.BlockSpec((depth, tile), lambda i, at: (0, i)),
                AT_SPEC,
            ),
            scratch_shapes=[
                pltpu.VMEM((depth, width + EXTRA), LOW),
                pltpu.VMEM((8, depth), F32),
                pltpu.SemaphoreType.DMA((1,)),
            ],
        ),
        compiler_params=params(),
        cost_estimate=cost(2 * height * depth * width),
    )(at, *after, rows, *pieces)


def slot_rows(lengths_ref, block, row_count):
    along = lax.broadcasted_iota(jnp.int32, (1, row_count), 1)
    down = lax.broadcasted_iota(jnp.int32, (row_count, 1), 0)
    bound, lane_slot, row_slot = 0, jnp.zeros_like(along), jnp.zeros_like(down)
    for slot in range(SLOTS):
        bound = bound + lengths_ref[block, slot]
        lane_slot = lane_slot + (along >= bound).astype(jnp.int32)
        row_slot = row_slot + (down >= bound).astype(jnp.int32)
    return lane_slot, row_slot


def query_rows(lane_slot):
    line = lax.broadcasted_iota(jnp.int32, (8, lane_slot.shape[1]), 0)
    return jnp.where(line == lane_slot, -BIG, 0.0)


def key_columns(row_slot, offset):
    column = lax.broadcasted_iota(jnp.int32, (row_slot.shape[0], 128), 1) - offset
    barred = (column >= 0) & (column <= SLOTS) & ((column != row_slot) | (row_slot == SLOTS))
    return jnp.where(barred, 1.0, 0.0).astype(LOW)


def attend_kernel(lengths_ref, at, q_ref, k_ref, v_ref, out_ref, turned_ref, log_ref, at_ref):
    hand_on(at, at_ref)
    block = pl.program_id(0) // (H // 2 // PAIRS)
    row_count = q_ref.shape[0]
    lane_slot, row_slot = slot_rows(lengths_ref, block, row_count)
    inside = lane_slot < SLOTS
    lane = lax.broadcasted_iota(jnp.int32, (row_count, 128), 1)
    barred = query_rows(lane_slot).astype(LOW)
    padded = jnp.concatenate([barred, jnp.zeros((HD - 8, row_count), LOW)], axis=0)
    for pair in range(PAIRS):
        attend_pair(
            pair, inside, lane, row_slot, padded, q_ref, k_ref, v_ref, out_ref, turned_ref, log_ref
        )


def attend_pair(pair, inside, lane, row_slot, padded, q_ref, k_ref, v_ref, out_ref, turned_ref, log_ref):
    row_count = q_ref.shape[0]
    columns = slice(pair * 128, (pair + 1) * 128)
    q_turned = (q_ref[:, columns].astype(F32) * SCALE).T.astype(LOW)
    v_turned = v_ref[:, columns].astype(F32).T
    v_low = v_turned.astype(LOW)
    ones = jnp.ones((16, row_count), LOW)
    results = []
    for head in range(2):
        own = (lane < HD) if head == 0 else (lane >= HD)
        keyed = jnp.where(own, k_ref[:, columns], key_columns(row_slot, HD * (1 - head)))
        half = q_turned[head * HD : (head + 1) * HD]
        query = jnp.concatenate([half, padded] if head == 0 else [padded, half], axis=0)
        scores = nn(keyed, query)
        highest = jnp.max(scores, axis=0, keepdims=True)
        weights = jnp.exp(scores - highest)
        low = weights.astype(LOW)
        values = jnp.concatenate([v_low[head * HD : (head + 1) * HD], ones], axis=0)
        mixed = nn(values, low)
        total = mixed[HD : HD + 1]
        result = mixed[:HD] / total
        results.append(jnp.where(inside, result, v_turned[head * HD : (head + 1) * HD]))
        log_ref[0, 2 * pair + head : 2 * pair + head + 1] = jnp.where(inside, highest + jnp.log(total), BIG)
    turned = jnp.concatenate(results, axis=0)
    turned_ref[columns] = turned.astype(LOW)
    out_ref[:, columns] = turned.T.astype(LOW)


def attend(at, lengths, projected, after=()):
    rows = projected.shape[0]
    blocks, pairs = rows // CAP, H // 2 // PAIRS
    width = H * HD

    def column(part):
        return pl.BlockSpec((CAP, 128 * PAIRS), lambda i, n, at: (i // pairs, part * pairs + i % pairs))

    return pl.pallas_call(
        later(attend_kernel, 2, after),
        out_shape=(
            jax.ShapeDtypeStruct((rows, width), LOW),
            jax.ShapeDtypeStruct((width, rows), LOW),
            jax.ShapeDtypeStruct((blocks * pairs, 8, CAP), F32),
            AT,
        ),
        grid_spec=pltpu.PrefetchScalarGridSpec(
            num_scalar_prefetch=2,
            grid=(blocks * pairs,),
            in_specs=[ANY] * len(after) + [column(0), column(1), column(2)],
            out_specs=(
                column(0),
                pl.BlockSpec((128 * PAIRS, CAP), lambda i, n, at: (i % pairs, i // pairs)),
                pl.BlockSpec((1, 8, CAP), lambda i, n, at: (i, 0, 0)),
                AT_SPEC,
            ),
        ),
        compiler_params=params(),
        cost_estimate=cost(4 * rows * CAP * width, 12),
    )(lengths, at, *after, projected, projected, projected)


def three(value):
    first = value.astype(LOW).astype(F32)
    rest = value - first
    second = rest.astype(LOW).astype(F32)
    return first, second, rest - second


def attend_back_kernel(lengths_ref, at, q_ref, k_ref, v_ref, att_ref, grad_ref, log_ref, dq_ref, dk_ref, dv_ref, sums_ref, at_ref):
    hand_on(at, at_ref)
    block, step = pl.program_id(0) // (H // 2 // PAIRS), pl.program_id(0) % (H // 2 // PAIRS)
    row_count = q_ref.shape[0]
    lane_slot, row_slot = slot_rows(lengths_ref, block, row_count)
    outside = lane_slot >= SLOTS
    lane = lax.broadcasted_iota(jnp.int32, (row_count, 128), 1)
    barred = query_rows(lane_slot)
    refs = (q_ref, k_ref, v_ref, att_ref, grad_ref, log_ref, dq_ref, dk_ref, dv_ref, sums_ref)

    @first_step
    def _():
        sums_ref[...] = jnp.zeros_like(sums_ref)

    for pair in range(PAIRS):
        attend_back_pair(pair, step, row_slot, outside, lane, barred, *refs)


def attend_back_pair(
    pair, step, row_slot, outside, lane, barred, q_ref, k_ref, v_ref, att_ref, grad_ref, log_ref, dq_ref, dk_ref, dv_ref, sums_ref
):
    row_count = q_ref.shape[0]
    columns = slice(pair * 128, (pair + 1) * 128)
    q_scaled = (q_ref[:, columns].astype(F32) * SCALE)
    q_turned = q_scaled.T.astype(LOW)
    k_scaled = k_ref[:, columns].astype(F32) * SCALE
    k_turned = k_scaled.T.astype(LOW)
    grad_wide = grad_ref[:, columns].astype(F32).T
    grad_turned = grad_wide
    mixed = grad_turned * att_ref[columns].astype(F32)
    grad_turned = grad_turned.astype(LOW)
    line = lax.broadcasted_iota(jnp.int32, (8, row_count), 0)
    none = jnp.zeros((HD - 16, row_count), F32)

    def lines(value):
        first, second, third = three(value)
        return jnp.where(
            line == 0, -first, jnp.where(line == 1, -second, jnp.where(line == 2, -third, 0.0))
        )

    dqs, dks, dvs = [], [], []
    for head in range(2):
        own = (lane < HD) if head == 0 else (lane >= HD)
        start = HD * (1 - head)
        unit = (lane >= start + 8) & (lane < start + 11)
        keyed = jnp.where(own, k_ref[:, columns], jnp.where(unit, jnp.ones((), LOW), key_columns(row_slot, start)))
        valued = jnp.where(own, v_ref[:, columns], jnp.where(unit, jnp.ones((), LOW), jnp.zeros((), LOW)))
        extra = jnp.concatenate([barred, lines(log_ref[0, 2 * pair + head : 2 * pair + head + 1]), none], axis=0).astype(LOW)
        half = slice(head * HD, (head + 1) * HD)
        query = jnp.concatenate([q_turned[half], extra] if head == 0 else [extra, q_turned[half]], axis=0)
        weights = jnp.exp(nn(keyed, query))
        inner = jnp.sum(mixed[half], axis=0, keepdims=True)
        extra = jnp.concatenate([jnp.zeros_like(barred), lines(inner), none], axis=0).astype(LOW)
        grad = jnp.concatenate([grad_turned[half], extra] if head == 0 else [extra, grad_turned[half]], axis=0)
        moved = (weights * nn(valued, grad)).astype(LOW)
        dvs.append(nt(grad_turned[half], weights.astype(LOW)))
        dks.append(nt(q_turned[half], moved))
        dqs.append(nn(k_turned[half], moved))
    dq = jnp.concatenate(dqs, axis=0).T.astype(LOW)
    dq_ref[:, columns] = dq
    dk_ref[:, columns] = jnp.concatenate(dks, axis=0).T.astype(LOW)
    dv = jnp.concatenate(dvs, axis=0)
    dv = jnp.where(outside, dv + grad_wide, dv).T.astype(LOW)
    dv_ref[:, columns] = dv

    span = pl.ds(pl.multiple_of((step * PAIRS + pair) * 128, 128), 128)
    sums_ref[0:1, span] += jnp.sum(dq.astype(F32), axis=0, keepdims=True)
    sums_ref[1:2, span] += jnp.sum(dv.astype(F32), axis=0, keepdims=True)


def attend_back(at, lengths, projected, turned, grad_attended, logs, after=()):
    rows = projected.shape[0]
    blocks, pairs = rows // CAP, H // 2 // PAIRS
    width = H * HD

    def column(part):
        return pl.BlockSpec((CAP, 128 * PAIRS), lambda i, n, at: (i // pairs, part * pairs + i % pairs))

    return pl.pallas_call(
        later(attend_back_kernel, 2, after),
        out_shape=(jax.ShapeDtypeStruct((rows, width), LOW),) * 3 + (jax.ShapeDtypeStruct((8, width), F32), AT),
        grid_spec=pltpu.PrefetchScalarGridSpec(
            num_scalar_prefetch=2,
            grid=(blocks * pairs,),
            in_specs=[ANY] * len(after)
            + [
                column(0), column(1), column(2),
                pl.BlockSpec((128 * PAIRS, CAP), lambda i, n, at: (i % pairs, i // pairs)),
                column(0),
                pl.BlockSpec((1, 8, CAP), lambda i, n, at: (i, 0, 0)),
            ],
            out_specs=(column(0),) * 3 + (pl.BlockSpec((8, width), lambda i, n, at: (0, 0)), AT_SPEC),
        ),
        compiler_params=params(),
        cost_estimate=cost(10 * rows * CAP * width, 5),
    )(lengths, at, *after, projected, projected, projected, turned, grad_attended, logs)


def norm(values):
    centre = jnp.mean(values, axis=-1, keepdims=True)
    centred = values - centre
    scale = lax.rsqrt(jnp.mean(centred * centred, axis=-1, keepdims=True) + EPSILON)
    return centred * scale, scale


def norm_back(grad, normal, scale):
    return scale * (
        grad
        - jnp.mean(grad, axis=-1, keepdims=True)
        - normal * jnp.mean(grad * normal, axis=-1, keepdims=True)
    )


ROOT_HALF = 0.7071067811865476
ROOT_TAU = 0.3989422804014327


def up_kernel(plan, chunk, at, rows_ref, att_ref, *refs):
    pieces = refs[:-11]
    (
        active_ref, slope_ref, normal_ref, scale_ref, first_ref, turned_ref, small_ref, at_ref, w_wide, wide_ref, sems,
    ) = refs[-11:]
    depth = w_wide.shape[0]
    hidden = w_wide.shape[1] - depth - EXTRA
    groups = [(pieces, w_wide, depth, False)]

    def load():
        hand_on(at, at_ref)
        fetch(plan, at, groups, sems)
        wait_for(plan, at, groups, sems, 0)
        table = w_wide[:, hidden + depth :].astype(F32).T
        small_ref[...] = table[:8]
        part = depth // plan.shards
        for shard in range(plan.shards):
            for line in range(hidden // depth):
                start = (shard * (hidden // depth) + line) * part
                wide_ref[0:1, start : start + part] = table[8 + line : 9 + line, shard * part : (shard + 1) * part]

    first_step(load)

    def small(index):
        return small_ref[index : index + 1]

    residual = rows_ref[...].astype(F32) + nn(att_ref[...], w_wide[:, hidden : hidden + depth]) + small(0)
    normal, scale = norm(residual)
    normal_ref[...] = normal.astype(LOW)
    scale_ref[...] = jnp.broadcast_to(scale, scale_ref.shape)
    first = normal * small(2) + small(3)
    first_ref[...] = first
    low = first.astype(LOW)
    turned_ref[...] = low.T
    for start in range(0, hidden, chunk):
        span = slice(start, start + chunk)
        wide = nn(low, w_wide[:, span]) + wide_ref[0:1, span]
        cumulative = 0.5 * (1.0 + lax.erf(wide * ROOT_HALF))
        active_ref[:, span] = (wide * cumulative).astype(LOW)
        slope_ref[:, span] = (cumulative + wide * (ROOT_TAU * jnp.exp(-0.5 * wide * wide))).astype(LOW)


def tiled(tile, width):
    return pl.BlockSpec((tile, width), lambda i, at: (i, 0))


def turned_tile(tile, width):
    return pl.BlockSpec((width, tile), lambda i, at: (0, i))


def whole_block(height, width):
    return pl.BlockSpec((height, width), lambda i, at: (0, 0))


def up(plan, at, rows, attended, hidden, pieces, tile=256, chunk=1024, after=()):
    height, depth = rows.shape
    return pl.pallas_call(
        later(functools.partial(up_kernel, plan, chunk), 1, after),
        out_shape=(
            jax.ShapeDtypeStruct((height, hidden), LOW),
            jax.ShapeDtypeStruct((height, hidden), LOW),
            jax.ShapeDtypeStruct((height, depth), LOW),
            jax.ShapeDtypeStruct((height, 128), F32),
            jax.ShapeDtypeStruct((height, depth), F32),
            jax.ShapeDtypeStruct((depth, height), LOW),
            jax.ShapeDtypeStruct((8, depth), F32),
            AT,
        ),
        grid_spec=pltpu.PrefetchScalarGridSpec(
            num_scalar_prefetch=1,
            grid=(height // tile,),
            in_specs=[ANY] * len(after) + [tiled(tile, depth), tiled(tile, depth)] + [ANY] * len(pieces),
            out_specs=(
                tiled(tile, hidden), tiled(tile, hidden), tiled(tile, depth), tiled(tile, 128),
                tiled(tile, depth), turned_tile(tile, depth), whole_block(8, depth), AT_SPEC,
            ),
            scratch_shapes=[
                pltpu.VMEM((depth, hidden + depth + EXTRA), LOW),
                pltpu.VMEM((8, hidden), F32),
                pltpu.SemaphoreType.DMA((1,)),
            ],
        ),
        compiler_params=params(),
        cost_estimate=cost(2 * height * depth * (depth + hidden)),
    )(at, *after, rows, attended, *pieces)


def over_kernel(plan, chunk, at, first_ref, active_ref, cot_ref, small_ref, *refs):
    pieces = refs[:-6]
    result_ref, second_ref, sums_ref, at_ref, w_contract, sems = refs[-6:]
    hidden = w_contract.shape[0]
    groups = [(pieces, w_contract, hidden, False)]

    def load():
        hand_on(at, at_ref)
        fetch(plan, at, groups, sems)
        sums_ref[...] = jnp.zeros_like(sums_ref)
        wait_for(plan, at, groups, sems, 0)

    first_step(load)

    def small(index):
        return small_ref[index : index + 1].astype(F32)

    def add(index, value):
        sums_ref[index : index + 1] += jnp.sum(value, axis=0, keepdims=True)

    normal, scale = norm(first_ref[...] + small(1) + nn(active_ref[...], w_contract[...]))
    result_ref[...] = (normal * small(4) + small(5)).astype(LOW)
    cot = cot_ref[...].astype(F32)
    add(4, cot * normal)
    add(5, cot)
    second = norm_back(cot * small(4), normal, scale).astype(LOW)
    second_ref[...] = second
    add(1, second.astype(F32))


def over(plan, at, first, active, cot, small, pieces, tile=256, chunk=1024, after=()):
    height, depth = first.shape
    hidden = active.shape[1]
    return pl.pallas_call(
        later(functools.partial(over_kernel, plan, chunk), 1, after),
        out_shape=(
            jax.ShapeDtypeStruct((height, depth), LOW),
            jax.ShapeDtypeStruct((height, depth), LOW),
            jax.ShapeDtypeStruct((8, depth), F32),
            AT,
        ),
        grid_spec=pltpu.PrefetchScalarGridSpec(
            num_scalar_prefetch=1,
            grid=(height // tile,),
            in_specs=[ANY] * len(after)
            + [tiled(tile, depth), tiled(tile, hidden), tiled(tile, depth), whole_block(8, depth)]
            + [ANY] * len(pieces),
            out_specs=(
                tiled(tile, depth), tiled(tile, depth), whole_block(8, depth), AT_SPEC,
            ),
            scratch_shapes=[pltpu.VMEM((hidden, depth), LOW), pltpu.SemaphoreType.DMA((1,))],
        ),
        compiler_params=params(),
        cost_estimate=cost(2 * height * depth * hidden),
    )(at, *after, first, active, cot, small, *pieces)


def down_kernel(plan, counts, chunk, at, second_ref, slope_ref, normal_ref, scale_ref, small_ref, *refs):
    first_count, second_count = counts
    wide_pieces, contract_pieces = refs[:first_count], refs[first_count : first_count + second_count]
    expanded_ref, branch_ref, grad_att_ref, sums_ref, wide_sums_ref, at_ref, w_wide, w_contract, sems = refs[
        first_count + second_count :
    ]
    hidden, depth = w_contract.shape

    groups = [(contract_pieces, w_contract, hidden, False), (wide_pieces, w_wide, depth, False)]

    def load():
        hand_on(at, at_ref)
        fetch(plan, at, groups, sems)
        sums_ref[...] = jnp.zeros_like(sums_ref)
        wide_sums_ref[...] = jnp.zeros_like(wide_sums_ref)
        wait_for(plan, at, groups, sems, 0)

    first_step(load)

    def add(index, value):
        sums_ref[index : index + 1] += jnp.sum(value, axis=0, keepdims=True)

    second = second_ref[...]
    total = second.astype(F32)
    for start in range(0, hidden, chunk):
        span = slice(start, start + chunk)
        grad = (nt(second, w_contract[span]) * slope_ref[:, span].astype(F32)).astype(LOW)
        expanded_ref[:, span] = grad
        wide_sums_ref[0:1, span] += jnp.sum(grad.astype(F32), axis=0, keepdims=True)
        if start == 0:
            first_step(lambda: wait_for(plan, at, groups, sems, 1))
        total = total + nt(grad, w_wide[:, span])
    normal = normal_ref[...].astype(F32)
    add(2, total * normal)
    add(3, total)
    branch = norm_back(total * small_ref[2:3].astype(F32), normal, scale_ref[:, 0:1]).astype(LOW)
    branch_ref[...] = branch
    add(0, branch.astype(F32))
    grad_att_ref[...] = nt(branch, w_wide[:, hidden : hidden + depth]).astype(LOW)


def down(plan, at, second, slope, normal, scale, small, wide_pieces, contract_pieces, tile=256, chunk=1024, after=()):
    height, depth = second.shape
    hidden = slope.shape[1]

    def tiled(width):
        return pl.BlockSpec((tile, width), lambda i, at: (i, 0))

    def whole(height, width):
        return pl.BlockSpec((height, width), lambda i, at: (0, 0))

    return pl.pallas_call(
        later(functools.partial(down_kernel, plan, (len(wide_pieces), len(contract_pieces)), chunk), 1, after),
        out_shape=(
            jax.ShapeDtypeStruct((height, hidden), LOW),
            jax.ShapeDtypeStruct((height, depth), LOW),
            jax.ShapeDtypeStruct((height, depth), LOW),
            jax.ShapeDtypeStruct((8, depth), F32),
            jax.ShapeDtypeStruct((8, hidden), F32),
            AT,
        ),
        grid_spec=pltpu.PrefetchScalarGridSpec(
            num_scalar_prefetch=1,
            grid=(height // tile,),
            in_specs=[ANY] * len(after)
            + [tiled(depth), tiled(hidden), tiled(depth), tiled(128), whole(8, depth)]
            + [ANY] * (len(wide_pieces) + len(contract_pieces)),
            out_specs=(tiled(hidden), tiled(depth), tiled(depth), whole(8, depth), whole(8, hidden), AT_SPEC),
            scratch_shapes=[
                pltpu.VMEM((depth, hidden + depth + EXTRA), LOW),
                pltpu.VMEM((hidden, depth), LOW),
                pltpu.SemaphoreType.DMA((2,)),
            ],
        ),
        compiler_params=params(),
        cost_estimate=cost(2 * height * depth * (depth + 2 * hidden)),
    )(at, *after, second, slope, normal, scale, small, *wide_pieces, *contract_pieces)


def source(at, flip, group, k):
    shard = (at[0] ^ k) * 4 + (at[1] ^ (group % 2)) * 2 + (at[2] ^ flip)
    return shard * 2 + (at[3] ^ (group // 2))


def outer_tall_kernel(at, left, right, out, at_ref):
    hand_on(at, at_ref)
    out[...] = tn(left[...], right[...]).astype(LOW)


def outer_tall(at, left, right, tile=512, after=()):
    height, rows = left.shape
    width = right.shape[1]
    return pl.pallas_call(
        later(outer_tall_kernel, 1, after),
        out_shape=(jax.ShapeDtypeStruct((rows, width), LOW), AT),
        grid_spec=pltpu.PrefetchScalarGridSpec(
            num_scalar_prefetch=1,
            grid=(rows // tile,),
            in_specs=[ANY] * len(after)
            + [pl.BlockSpec((height, tile), lambda i, at: (0, i)), whole_block(height, width)],
            out_specs=(tiled(tile, width), AT_SPEC),
        ),
        compiler_params=params(),
        cost_estimate=cost(2 * height * rows * width),
    )(at, *after, left, right)


def outer_row_kernel(count, tile, at, turned, extra, *refs):
    rights, (out, at_ref) = refs[:count], refs[count:]
    step = pl.program_id(0)
    total = out.shape[1] - EXTRA
    steps = total // tile // count
    for place in range(count * steps):

        @pl.when(step == place)
        def _(place=place):
            out[:, place * tile : (place + 1) * tile] = nn(turned[...], rights[place // steps][...]).astype(LOW)

    @first_step
    def _():
        hand_on(at, at_ref)
        lines = jnp.zeros((EXTRA - extra.shape[0], extra.shape[1]), F32)
        out[:, total:] = jnp.concatenate([extra[...], lines], axis=0).T.astype(LOW)


def outer_row(at, turned, rights, extra, tile=512, after=()):
    rows, height = turned.shape
    steps = rights[0].shape[1] // tile
    count = len(rights)
    width = count * steps * tile

    def column(index):
        return pl.BlockSpec((height, tile), lambda i, at: (0, jnp.clip(i - index * steps, 0, steps - 1)))

    return pl.pallas_call(
        later(functools.partial(outer_row_kernel, count, tile), 1, after),
        out_shape=(jax.ShapeDtypeStruct((rows, width + EXTRA), LOW), AT),
        grid_spec=pltpu.PrefetchScalarGridSpec(
            num_scalar_prefetch=1,
            grid=(count * steps,),
            in_specs=[ANY] * len(after)
            + [whole_block(rows, height), whole_block(*extra.shape)]
            + [column(index) for index in range(count)],
            out_specs=(whole_block(rows, width + EXTRA), AT_SPEC),
        ),
        compiler_params=params(),
        cost_estimate=cost(2 * height * rows * width),
    )(at, *after, turned, extra, *rights)


def outer_wide_kernel(flip, owners, firsts, tile, extra, at, *refs):
    count = max(owners) + 1
    turned, rights = refs[:count], refs[count : count + len(owners)]
    if extra:
        extra_ref, out, at_ref, lines, held, sem = refs[-6:]
    else:
        out, at_ref, held, sem = refs[-4:]
    step = pl.program_id(0)
    half = held.shape[1] // 16

    def load():
        hand_on(at, at_ref)
        copies = []
        for index, ref in enumerate(turned):
            for group in range(4):
                for k in range(4):
                    row = pl.multiple_of(source(at, flip, group, k) * half, half)
                    copies.append(
                        pltpu.make_async_copy(
                            ref.at[pl.ds(row, half)], held.at[index, pl.ds((group * 4 + k) * half, half)], sem
                        )
                    )
        for copy in copies:
            copy.start()
        for copy in copies:
            copy.wait()

    first_step(load)
    if extra:
        @first_step
        def _():
            rest = jnp.zeros((EXTRA - extra_ref.shape[0], extra_ref.shape[1]), F32)
            lines[...] = jnp.concatenate([extra_ref[...], rest], axis=0).T.astype(LOW)
            for group in range(4):
                for k in range(4):
                    row = pl.multiple_of(source(at, flip, group, k) * half, half)
                    out[group * 4 + k, :, tile * firsts[-1] :] = lines[pl.ds(row, half), :]

    for index, owner in enumerate(owners):
        if extra:
            for place in range(firsts[index], firsts[index + 1]):

                @pl.when(step == place)
                def _(index=index, owner=owner, place=place):
                    result = nn(held[owner], rights[index][...]).astype(LOW)
                    out[:, :, place * tile : (place + 1) * tile] = result.reshape(16, half, tile)

            continue

        @pl.when((step >= firsts[index]) & (step < firsts[index + 1]))
        def _(index=index, owner=owner):
            result = nn(held[owner], rights[index][...]).astype(LOW)
            out[...] = result.reshape(out.shape)


def outer_wide(at, turned, rights, owners, flip, tile=1024, extra=None, after=()):
    rows, height = turned[0].shape
    half = rows // 32
    counts = [right.shape[1] // tile for right in rights]
    firsts = [sum(counts[:i]) for i in range(len(counts) + 1)]
    width = tile * firsts[-1]
    more = [] if extra is None else [extra]
    wide = width + EXTRA * len(more)
    block = pl.BlockSpec((16, half, tile), lambda i, at: (0, 0, i))
    if more:
        block = pl.BlockSpec((16, half, wide), lambda i, at: (0, 0, 0))

    def column(index):
        return pl.BlockSpec((height, tile), lambda i, at: (0, jnp.clip(i - firsts[index], 0, counts[index] - 1)))

    return pl.pallas_call(
        later(functools.partial(outer_wide_kernel, flip, tuple(owners), tuple(firsts), tile, bool(more)), 1, after),
        out_shape=(jax.ShapeDtypeStruct((16, half, wide), LOW), AT),
        grid_spec=pltpu.PrefetchScalarGridSpec(
            num_scalar_prefetch=1,
            grid=(firsts[-1],),
            in_specs=[ANY] * len(after)
            + [ANY] * len(turned)
            + [column(index) for index in range(len(rights))]
            + [whole_block(*line.shape) for line in more],
            out_specs=(block, AT_SPEC),
            scratch_shapes=[pltpu.VMEM((rows, EXTRA), LOW) for line in more]
            + [pltpu.VMEM((len(turned), rows // 2, height), LOW), pltpu.SemaphoreType.DMA],
        ),
        compiler_params=params(),
        cost_estimate=cost(height * rows * width),
    )(at, *after, *turned, *rights, *more)


def owned_sum(whole):
    return lax.psum_scatter(whole, "fsdp", scatter_dimension=0, tiled=True)


def copies_sum(plan, at, owned):
    if plan.copies == 2:
        owned = owned + at[4].astype(LOW)
        return owned.astype(F32) + plan.other_copy(owned).astype(F32)
    return lax.psum(owned, "rep").astype(F32)


def back_kernel(plan, count, at, branch_ref, dq_ref, dk_ref, dv_ref, *refs):
    pieces, (out_ref, at_ref, weight, sems) = refs[:count], refs[count:]
    width = dq_ref.shape[1]

    def load():
        hand_on(at, at_ref)
        groups = [(pieces, weight, weight.shape[0], True)]
        fetch(plan, at, groups, sems)
        wait_for(plan, at, groups, sems, 0)

    first_step(load)

    total = branch_ref[...].astype(F32)
    for index, ref in enumerate((dq_ref, dk_ref, dv_ref)):
        total = total + nt(ref[...], weight[:, index * width : (index + 1) * width])
    out_ref[...] = total.astype(LOW)


def back(plan, at, branch, dq, dk, dv, pieces, tile=256, after=()):
    count = len(pieces)
    height, depth = branch.shape
    width = dq.shape[1]
    tiled = pl.BlockSpec((tile, depth), lambda i, at: (i, 0))
    return pl.pallas_call(
        later(functools.partial(back_kernel, plan, count), 1, after),
        out_shape=(jax.ShapeDtypeStruct((height, depth), LOW), AT),
        grid_spec=pltpu.PrefetchScalarGridSpec(
            num_scalar_prefetch=1,
            grid=(height // tile,),
            in_specs=[ANY] * len(after)
            + [tiled] * 4 + [ANY] * count,
            out_specs=(tiled, AT_SPEC),
            scratch_shapes=[pltpu.VMEM((depth, 3 * width + EXTRA), LOW), pltpu.SemaphoreType.DMA((1,))],
        ),
        compiler_params=params(),
        cost_estimate=cost(6 * height * depth * width),
    )(at, *after, branch, dq, dk, dv, *pieces)


def body(
    tokens, seq_lengths, out_cotangent, project_in, project_out, expand, contract,
    query_bias, value_bias, out_bias, expand_bias, contract_bias,
    first_gain, first_shift, second_gain, second_shift,
    *, shards, copies,
):
    plan = Plan(shards, copies)
    at = place()
    depth = tokens.shape[1]
    hidden = expand.shape[1]
    part, wide_part = query_bias.shape[0], expand_bias.shape[0]

    def columns(*vectors):
        table = jnp.stack([vector for vector in vectors], axis=1)
        return jnp.pad(table, ((0, 0), (0, EXTRA - len(vectors))))

    zero = jnp.zeros_like(query_bias)
    in_shard = jnp.concatenate([project_in, columns(query_bias, value_bias)], axis=1)
    wide_bias = tuple(expand_bias[i * part : (i + 1) * part] for i in range(wide_part // part))
    small = (out_bias, contract_bias, first_gain, first_shift, second_gain, second_shift, zero, zero)
    wide_shard = jnp.concatenate([expand, project_out, columns(*small, *wide_bias)], axis=1)
    width = project_in.shape[1]
    if plan.split:
        in_beside, in_parts = plan.gather_z(at, in_shard, True)
        in_far, in_across, in_other = plan.gather_xy(at, in_shard, in_parts, True)
        unused, wide_parts = plan.gather_z(pinned(at, in_parts[2]), wide_shard)
        in_corners = plan.gather_corner(at, in_shard, in_across, in_other, True)
        in_main = (in_shard, in_beside, in_far, in_across, in_other)
        at_wide = pinned(at, *wide_parts)
        in_cores = plan.gather_core(at, *in_main) + plan.gather_core(at_wide, *in_corners)
        in_pieces = list(in_main + in_corners) + in_cores
        at_core = at_wide
        wide_far, wide_across, wide_other = plan.gather_xy(at_core, wide_shard, wide_parts)
        contract_pieces = [lax.all_gather(contract + pinned(at_core, wide_across, wide_other)[4].astype(LOW), "fsdp", axis=0, tiled=True)]
        wide_corners = plan.gather_corner(at_core, wide_shard, wide_across, wide_other)
    else:
        in_pieces, wide_pieces, contract_pieces = (
            [lax.all_gather(shard, "fsdp", axis=0, tiled=True)] for shard in (in_shard, wide_shard, contract)
        )
    first_after = [wide_across, wide_other] if plan.split else []
    projected, tokens_turned, at = project(plan, at, tokens, in_pieces, depth, width, after=first_after)
    if plan.split:
        wide_main = (wide_shard, wide_far, wide_across, wide_other)
        attended, attended_turned, logs, at = attend(at, seq_lengths, projected, after=wide_corners)
        wide_pieces = list(wide_main + wide_corners)
        wide_pieces += plan.gather_core(at, *wide_main) + plan.gather_core(at, *wide_corners)
    else:
        attended, attended_turned, logs, at = attend(at, seq_lengths, projected)
    active, slope, normal, scale, first, first_turned, table, at = up(plan, at, tokens, attended, hidden, wide_pieces)
    result, second, sums, at = over(plan, at, first, active, out_cotangent, table, contract_pieces)
    whole, at = outer_tall(at, active, second)
    contract_owned = owned_sum(whole)
    grad_expanded, branch, grad_attended, more_sums, wide_sums, at = down(
        plan, at, second, slope, normal, scale, table, wide_pieces, contract_pieces
    )
    lines = wide_sums[0].reshape(shards, wide_part // part, part).transpose(1, 0, 2).reshape(-1, depth)
    lines = jnp.concatenate([sums[:6] + more_sums[:6], lines], axis=0)
    lines = jnp.pad(lines, ((0, 14 - lines.shape[0]), (0, 0)))
    if plan.split:
        turned, rights, owners = (first_turned, attended_turned), (grad_expanded, branch), (0, 1)
        theirs, at = outer_wide(at, turned, rights, owners, 1)
        e_got = plan.flip(theirs, 1)
        e_mine, at = outer_wide(at, turned, rights, owners, 0)
        e_corners = plan.scatter_corner(at, e_mine, e_got)
        dq, dk, dv, back_sums, at = attend_back(at, seq_lengths, projected, attended_turned, grad_attended, logs)
        e_across, e_other = plan.scatter_xy(at, e_mine, e_got, *e_corners)
        extra = jnp.concatenate([back_sums[:2], lines], axis=0)
        turned, rights, owners = (tokens_turned,), (dq, dk, dv), (0, 0, 0)
        theirs, at = outer_wide(at, turned, rights, owners, 1, extra=extra, after=e_corners)
        i_got = plan.flip(theirs, 1)
        i_mine, at = outer_wide(at, turned, rights, owners, 0, extra=extra, after=[contract_owned])
        contract_sum = copies_sum(plan, at, contract_owned)
        e_parts = plan.scatter_z(at, e_mine, e_got, e_across, e_other)
        i_corners = plan.scatter_corner(at, i_mine, i_got)
        grad_tokens, at = back(plan, at, branch, dq, dk, dv, in_pieces, after=[i_got])
        i_across, i_other = plan.scatter_xy(at, i_mine, i_got, *i_corners)
        e_ends = plan.scatter_end(at, e_parts)
        i_parts = plan.scatter_z(at, i_mine, i_got, i_across, i_other)
        owned = jnp.concatenate(plan.scatter_end(at, i_parts), axis=0)
        grad_wide = jnp.concatenate(e_ends, axis=0)
        grad_expand, grad_project_out = grad_wide[:, :hidden], grad_wide[:, hidden:]
    else:
        none = jnp.zeros((8, depth), F32)
        whole, at = outer_row(at, first_turned, (grad_expanded,), none)
        grad_expand = copies_sum(plan, at, owned_sum(whole))[:, :hidden]
        whole, at = outer_row(at, attended_turned, (branch,), none)
        grad_project_out = copies_sum(plan, at, owned_sum(whole))[:, :depth]
        dq, dk, dv, back_sums, at = attend_back(at, seq_lengths, projected, attended_turned, grad_attended, logs)
        extra = jnp.concatenate([back_sums[:2], lines], axis=0)
        whole, at = outer_row(at, tokens_turned, (dq, dk, dv), extra)
        owned = copies_sum(plan, at, owned_sum(whole))
        contract_sum = copies_sum(plan, at, contract_owned)
        grad_tokens, at = back(plan, at, branch, dq, dk, dv, in_pieces)
    grad_contract = contract_sum
    grad_project_in = owned[:, :width]
    small = owned[:, width : width + 8 + wide_part // part].T
    grad_query, grad_value, grad_out, grad_down, gain_one, shift_one, gain_two, shift_two = (small[i] for i in range(8))
    grad_wide_bias = small[8:].reshape(-1)
    return (
        result, grad_tokens, grad_project_in, grad_project_out, grad_expand, grad_contract,
        grad_query, grad_value, grad_out, grad_wide_bias, grad_down,
        gain_one, shift_one, gain_two, shift_two,
    )


def solution(mesh):
    split, row, vector = P(("fsdp", "rep"), None), P("fsdp", None), P("fsdp")
    return jax.shard_map(
        functools.partial(body, shards=mesh.shape["fsdp"], copies=mesh.shape["rep"]),
        mesh=mesh,
        in_specs=(split,) * 3 + (row,) * 4 + (vector,) * 9,
        out_specs=(split,) * 2 + (row,) * 4 + (vector,) * 9,
        check_vma=False,
    )
```
